512 devices in a mesh: ctx: 16 (over x, z_hi, core), head: 32 (over y, z_lo).
Axes of the slice: x: 4, y: 4, z: 16 (z_hi: 2, z_lo: 8; z = z_hi * 8 + z_lo), core: 2. Of those that a mesh axis runs over, the one named last changes fastest.
Arguments:
- queries: bfloat16 [128, 24576], P('ctx', 'head'), may hold values from -8 to 8
- w_uk: bfloat16 [128, 128, 512], P('head'), may hold values from -0.5 to 0.5
- value_up_weight: bfloat16 [128, 512, 128], P('head'), may hold values from -1 to 1
- w_out: bfloat16 [16384, 7168], P('head', 'ctx'), may hold values from -0.046875 to 0.046875
- kv_cache: bfloat16 [1024, 36864], P('ctx'), may hold values from -8 to 8
- blocks: int32 [128, 32], replicated, may hold values from 0 to 1023, as said below
Outputs:
- attended: bfloat16 [128, 7168], P('head', 'ctx')
The draws below stay inside these ranges and needn't reach their ends.
Inputs may be any that keep to these rules, and one draw needn't show every extreme that they name: Each row names 32 different blocks; at most 4 of a row's blocks lie in one shard of 64 blocks, and every row has exactly 4 in some shard.
All inputs are finite; a program needn't handle non-finite values.
Results may differ from the reference program's by a relative error of at most 0.011.
Values may be sent and summed in bfloat16 or wider, within the bound.
No kernel may reach another device: no remote copies, remote signals or barrier semaphores. Data moves between devices by JAX's collectives and lax.ppermute only.
A program may use at most 64 MiB of HBM per device.

```python
import jax
import jax.numpy as jnp
from jax import lax

D = 7168
H = 128
NOPE = 128
ROPE = 64
KVR = 512
VD = 128
BLOCK = 64
SEL = 32
BLK_DEV = 64
Q_TOT = 128
NBLK = 1024
CAP = 4
N_CTX = 16


def draw_queries(key, part):
    key = jax.random.fold_in(key, 1)
    shape = (Q_TOT, H, NOPE + ROPE)
    full = jnp.clip(jax.random.normal(key, shape, jnp.float32), -6.0, 6.0)
    return full.reshape(Q_TOT, H * (NOPE + ROPE)).astype(jnp.bfloat16)


def draw_kv_cache(key, part):
    key = jax.random.fold_in(key, 2)
    shape = (NBLK, BLOCK, KVR + ROPE)
    full = jnp.clip(jax.random.normal(key, shape, jnp.float32), -6.0, 6.0)
    return full.reshape(NBLK, BLOCK * (KVR + ROPE)).astype(jnp.bfloat16)


def draw_blocks(key, part):
    key = jax.random.fold_in(key, 7)
    shards = NBLK // BLK_DEV
    slots = shards * CAP
    first_key, second_key, third_key = jax.random.split(key, 3)
    noise = jax.random.randint(first_key, (Q_TOT, shards, CAP), 0, 65536, jnp.int32)
    favoured = jax.random.randint(third_key, (Q_TOT,), 0, shards, jnp.int32)
    shard_iota = jnp.arange(shards, dtype=jnp.int32)
    favour = shard_iota[None, :] * 2048 + jnp.where(shard_iota[None, :] == favoured[:, None], 4194304, 0).astype(jnp.int32)
    ranked = (noise + favour[:, :, None]).reshape(Q_TOT, slots) * slots + jnp.arange(slots, dtype=jnp.int32)[None, :]
    unused, chosen_slots = jax.lax.top_k(ranked, SEL)
    chosen_slots = chosen_slots.astype(jnp.int32)
    shard_of = chosen_slots // CAP
    rank_of = chosen_slots % CAP
    shuffle = jax.random.randint(second_key, (Q_TOT, shards, BLK_DEV), 0, 1048576, jnp.int32) * BLK_DEV
    shuffle = shuffle + jnp.arange(BLK_DEV, dtype=jnp.int32)[None, None, :]
    orders = jnp.argsort(shuffle, axis=-1).astype(jnp.int32).reshape(Q_TOT, shards * BLK_DEV)
    picked = jnp.take_along_axis(orders, shard_of * BLK_DEV + rank_of, axis=1)
    return (shard_of * BLK_DEV + picked).astype(jnp.int32)


def levels(key, shape, cuts, least, largest):
    level = 1.0
    for dim, shards_of in cuts:
        draws = jax.random.uniform(jax.random.fold_in(jax.random.fold_in(key, 6), dim), (shards_of,), jnp.float32, least / len(cuts), largest / len(cuts))
        level = level * jnp.repeat(jnp.exp(draws), shape[dim] // shards_of).reshape((-1,) + (1,) * (len(shape) - 1 - dim))
    return level


def scatter_about(key, extent, deviation, most, cuts=(), kind=jnp.bfloat16):
    gain = levels(key, extent, cuts, -0.22, 0.18) if cuts else 1.0
    values = jax.random.normal(key, extent, jnp.float32) * deviation * gain
    return jnp.minimum(jnp.maximum(values, -most), most).astype(kind)


def setup_inputs(seed: int = 0) -> dict:
    keys = jax.random.split(jax.random.key(seed), 7)
    queries = draw_queries(jax.random.fold_in(keys[6], 71), 0)
    w_uk = scatter_about(keys[1], (H, NOPE, KVR), NOPE ** -0.5, 0.5, ((0, 32),))
    value_up_weight = scatter_about(keys[2], (H, KVR, VD), (KVR // 16) ** -0.5, 1.0, ((0, 32),))
    w_out = scatter_about(keys[3], (H * VD, D), (H * VD) ** -0.5, 0.046875, ((0, 32), (1, 16)))
    kv_cache = draw_kv_cache(jax.random.fold_in(keys[6], 71), 0)
    blocks = draw_blocks(jax.random.fold_in(keys[6], 71), 0)
    return {"queries": queries, "w_uk": w_uk, "value_up_weight": value_up_weight, "w_out": w_out, "kv_cache": kv_cache, "blocks": blocks}


NEG_FILL = -1e30


def reference(queries, w_uk, value_up_weight, w_out, kv_cache, blocks):
    query_key_width = NOPE + ROPE
    key_width = KVR + ROPE
    scaling = query_key_width ** -0.5
    grouped = queries.reshape(Q_TOT, H, query_key_width)
    latent_q = jnp.einsum('rhn,hnk->rhk', grouped[:, :, :NOPE].astype(jnp.float32), w_uk.astype(jnp.float32)).astype(jnp.bfloat16)
    absorbed = jnp.concatenate([latent_q, grouped[:, :, NOPE:]], axis=-1)
    cache_tiles = kv_cache.reshape(NBLK, BLOCK, key_width)
    shard_ids = jnp.arange(N_CTX, dtype=jnp.int32)

    def one_row(operands):
        query_row, block_row = operands
        key_tiles = cache_tiles[block_row]
        flat_keys = key_tiles.reshape(SEL * BLOCK, key_width)
        scores = jnp.dot(query_row, flat_keys.T, preferred_element_type=jnp.float32) * scaling
        scores = scores.reshape(H, SEL, BLOCK)
        owner_shard = (block_row // BLK_DEV).astype(jnp.int32)
        member = owner_shard[None, :] == shard_ids[:, None]
        block_top = jnp.max(scores, axis=2)
        shard_top = jnp.max(jnp.where(member[None, :, :], block_top[:, None, :], NEG_FILL), axis=2)
        owner_top = jnp.take(shard_top, owner_shard, axis=1)
        weights = jnp.exp(scores - owner_top[:, :, None]).astype(jnp.bfloat16)
        overall = jnp.max(shard_top, axis=1)
        factor = jnp.exp(owner_top - overall[:, None])
        scaled = weights.astype(jnp.float32) * factor[:, :, None]
        row_total = jnp.sum(scaled, axis=(1, 2))
        values = flat_keys[:, :KVR].astype(jnp.float32)
        summed_values = jnp.dot(scaled.reshape(H, SEL * BLOCK), values, precision=lax.Precision.HIGHEST)
        return summed_values / row_total[:, None]

    latent_output_rows = lax.map(one_row, (absorbed, blocks))
    value_output_rows = jnp.einsum('dng,ngm->dnm', latent_output_rows, value_up_weight.astype(jnp.float32), precision=lax.Precision.HIGHEST).astype(jnp.bfloat16)
    value_output_rows = value_output_rows.reshape(Q_TOT, H * VD)
    return jnp.dot(value_output_rows, w_out, preferred_element_type=jnp.float32).astype(jnp.bfloat16)
```

```python
import numpy as np
import jax
import jax.numpy as jnp
from jax import lax
from jax.experimental import pallas as pl
from jax.experimental.pallas import tpu as pltpu
from jax.sharding import PartitionSpec as P

BF = jnp.bfloat16
F32 = jnp.float32
NEG = -1e30
H_DEV = 4
ROWS = 128
NOPE = 128
ROPE = 64
KVR = 512
VD = 128
BLOCK = 64
WIDE = 640
PAIR = 1152
QUAD = 4
COEF = float((NOPE + ROPE) ** -0.5 * np.log2(np.e))
INTERPRET = False

SAME_CORE = [[x * 4 + z * 2 + c for x in range(4) for z in range(2)] for c in range(2)]
SAME_CHIP = [[x * 4 + z * 2 + c for c in range(2)] for x in range(4) for z in range(2)]
SAME_HALF = [[x * 4 + z * 2 + c for c in range(2) for x in range(4)] for z in range(2)]


def nt_dot(a, b):
    return lax.dot_general(a, b, (((1,), (1,)), ((), ())), preferred_element_type=F32)


def dot(a, b):
    return jnp.dot(a, b, preferred_element_type=F32)


def pieces(x, n):
    out = []
    for _ in range(n):
        part = x.astype(BF).astype(F32)
        out.append(part)
        x = x - part
    return out


def with_stats(tops, totals, rows):
    lane = lax.broadcasted_iota(jnp.int32, (rows, 128), 1)
    tail = jnp.zeros((rows, 128), F32)
    for h in range(H_DEV):
        cols = pieces(tops[h], 3) + pieces(totals[h], 2)
        for k, col in enumerate(cols):
            tail = jnp.where(lane == 8 * h + k, col, tail)
    return tail


def stats_of(tail, h):
    t = tail[:, 8 * h : 8 * h + 8]
    top = t[:, 0:1] + (t[:, 1:2] + t[:, 2:3])
    return top, t[:, 3:4] + t[:, 4:5]


def attend(q_ref, we_ref, wo_ref, vue_ref, vuo_ref, bias_ref, kv_ref, out_ref, qe, qo, s_ref, p_ref):
    n_pairs = kv_ref.shape[1] // PAIR
    n_groups = n_pairs // QUAD
    for h in range(H_DEV):
        start = (h // 2) * 384 + (h % 2) * 128
        qs = q_ref[:, start : start + 256]
        qe[h * ROWS : (h + 1) * ROWS, :] = dot(qs, we_ref[h]).astype(BF)
        qo[h * ROWS : (h + 1) * ROWS, :] = dot(qs, wo_ref[h]).astype(BF)
    bias = jnp.concatenate([bias_ref[...]] * H_DEV, axis=0)

    top = jnp.full((H_DEV * ROWS, 128), NEG, F32)
    chunk = QUAD * BLOCK
    for i in range(n_groups):
        for odd in range(2):
            s = nt_dot((qe, qo)[odd][...], kv_slice(kv_ref, i, odd, WIDE))
            for part in range(chunk // 128):
                piece = s[:, part * 128 : (part + 1) * 128] + bias
                top = jnp.maximum(top, piece)
                at = (odd * n_groups + i) * chunk + part * 128
                s_ref[:, at : at + 128] = piece
    top = jnp.max(top, axis=1, keepdims=True)
    total = jnp.zeros((H_DEV * ROWS, 128), F32)
    for at in range(0, s_ref.shape[1], 128):
        w = jnp.exp2((s_ref[:, at : at + 128] - top) * COEF)
        total = total + w
        p_ref[:, at : at + 128] = w.astype(BF)
    total = jnp.sum(total, axis=1, keepdims=True)
    acc = [jnp.zeros((H_DEV * ROWS, KVR), F32), jnp.zeros((H_DEV * ROWS, WIDE), F32)]
    for odd in range(2):
        values = jnp.concatenate(
            [kv_slice(kv_ref, i, odd, (KVR, WIDE)[odd]) for i in range(n_groups)], axis=0
        )
        half = n_groups * chunk
        acc[odd] = dot(p_ref[:, odd * half : (odd + 1) * half], values).astype(BF)
    tops, totals = [], []
    for h in range(H_DEV):
        rows = slice(h * ROWS, (h + 1) * ROWS)
        z = dot(acc[0][rows], vue_ref[h]) + dot(acc[1][rows], vuo_ref[h])
        out_ref[:, h * VD : (h + 1) * VD] = z.astype(BF)
        tops.append(top[rows])
        totals.append(total[rows])
    out_ref[:, H_DEV * VD :] = with_stats(tops, totals, ROWS).astype(BF)


def kv_slice(kv_ref, i, odd, width):
    starts = [(i * QUAD + t) * PAIR + odd * KVR for t in range(QUAD)]
    return jnp.concatenate([kv_ref[:, s : s + width] for s in starts], axis=0)


def merge(parts, tails):
    nums, tops, totals = [], [], []
    for h in range(H_DEV):
        stats = [stats_of(t, h) for t in tails]
        top = stats[0][0]
        for m, _ in stats[1:]:
            top = jnp.maximum(top, m)
        num, total = 0.0, 0.0
        for part, (m, l) in zip(parts, stats):
            f = jnp.exp2((m - top) * COEF)
            num = num + part[:, h * VD : (h + 1) * VD] * f
            total = total + l * f
        nums.append(num)
        tops.append(top)
        totals.append(total)
    return nums, tops, totals


def merge_half(in_ref, out_ref):
    n, rows, _ = in_ref.shape
    data = [in_ref[s].astype(F32) for s in range(n)]
    nums, tops, totals = merge([d[:, : H_DEV * VD] for d in data], [d[:, H_DEV * VD :] for d in data])
    whole = jnp.concatenate(nums + [with_stats(tops, totals, rows)], axis=1).astype(BF)
    for k in range(out_ref.shape[0]):
        out_ref[k] = whole


def project(in_ref, w_ref, out_ref):
    groups = in_ref.shape[0] // 2
    data = [
        jnp.concatenate([in_ref[2 * g + z].astype(F32) for g in range(groups)], axis=0)
        for z in range(2)
    ]
    nums, _, totals = merge([d[:, : H_DEV * VD] for d in data], [d[:, H_DEV * VD :] for d in data])
    value = jnp.concatenate([n / t for n, t in zip(nums, totals)], axis=1).astype(BF)
    res = dot(value, w_ref[...])
    order = [res[(c * 8 + xz) * 8 : (c * 8 + xz) * 8 + 8] for xz in range(8) for c in range(2)]
    out_ref[...] = jnp.concatenate(order, axis=0).astype(BF)


def call(kernel, out_shape, *args, scratch=(), limit=16):
    return pl.pallas_call(
        kernel,
        out_shape=out_shape,
        in_specs=[pl.BlockSpec(memory_space=pltpu.VMEM)] * len(args),
        out_specs=pl.BlockSpec(memory_space=pltpu.VMEM),
        scratch_shapes=list(scratch),
        compiler_params=pltpu.CompilerParams(vmem_limit_bytes=limit * 2**20),
        interpret=INTERPRET,
    )(*args)


def spread(chunks, axis, groups):
    return lax.all_to_all(chunks, axis, 0, 0, axis_index_groups=groups)


def body(queries, w_uk, value_up_weight, w_out, kv_cache, blocks):
    own_rows = queries.shape[0]
    n_blocks = kv_cache.shape[0]
    q = spread(jnp.broadcast_to(queries[None], (8,) + queries.shape), "ctx", SAME_CORE)
    q = lax.all_gather(q.reshape(8 * own_rows, -1), "ctx", axis=0, tiled=True, axis_index_groups=SAME_CHIP)

    eye = jnp.broadcast_to(jnp.eye(ROPE, dtype=BF)[None], (H_DEV, ROPE, ROPE))

    def extended(lead):
        nope = jnp.pad(w_uk, ((0, 0), (0, 0), (lead, WIDE - KVR - lead)))
        rope = jnp.pad(eye, ((0, 0), (0, 0), (lead + KVR, WIDE - KVR - ROPE - lead)))
        both = jnp.concatenate([nope, rope], axis=1).reshape(H_DEV // 2, 2, NOPE + ROPE, WIDE)
        zero = jnp.zeros_like(both[:, 0, :ROPE])
        first = jnp.concatenate([both[:, 0], zero], axis=1)
        second = jnp.concatenate([zero, both[:, 1]], axis=1)
        return jnp.stack([first, second], axis=1).reshape(H_DEV, 256, WIDE)

    vu_odd = jnp.pad(value_up_weight, ((0, 0), (ROPE, ROPE), (0, 0)))
    picked = blocks.reshape(4, 2, 2, own_rows, -1).transpose(2, 0, 1, 3, 4).reshape(ROWS, -1)
    offsets = picked - lax.axis_index("ctx") * n_blocks
    lane = jnp.arange(2 * n_blocks, dtype=jnp.int32) % n_blocks
    present = jnp.any(offsets[:, :, None] == lane[None, None, :], axis=1)
    bias = jnp.where(present, 0.0, NEG).astype(F32)

    n_keys = n_blocks * BLOCK
    parts = call(
        attend,
        jax.ShapeDtypeStruct((ROWS, WIDE), BF),
        q, extended(0), extended(ROPE), value_up_weight, vu_odd, bias, kv_cache,
        scratch=[
            pltpu.VMEM((H_DEV * ROWS, WIDE), BF),
            pltpu.VMEM((H_DEV * ROWS, WIDE), BF),
            pltpu.VMEM((H_DEV * ROWS, n_keys), F32),
            pltpu.VMEM((H_DEV * ROWS, n_keys), BF),
        ],
        limit=40,
    )
    parts = spread(parts.reshape(8, 2 * own_rows, WIDE), "ctx", SAME_HALF)
    halves = call(merge_half, jax.ShapeDtypeStruct((8, 2 * own_rows, WIDE), BF), parts)
    halves = spread(halves, "ctx", SAME_CORE)
    halves = lax.all_gather(halves, "ctx", axis=0, tiled=True, axis_index_groups=SAME_CHIP)
    partial = call(project, jax.ShapeDtypeStruct((ROWS, w_out.shape[1]), BF), halves, w_out)
    n_head = lax.axis_size("head")
    pieces_in = lax.all_to_all(partial.reshape(n_head, ROWS // n_head, -1), "head", 0, 0)
    return jnp.sum(pieces_in.astype(F32), axis=0).astype(BF)


def solution(mesh):
    return jax.shard_map(
        body,
        mesh=mesh,
        in_specs=(
            P("ctx", "head"),
            P("head", None, None),
            P("head", None, None),
            P("head", "ctx"),
            P("ctx", None),
            P(),
        ),
        out_specs=P("head", "ctx"),
        check_vma=False,
    )
```

```python
import numpy as np
import jax
import jax.numpy as jnp
from jax import lax
from jax.experimental import pallas as pl
from jax.experimental.pallas import tpu as pltpu
from jax.sharding import PartitionSpec as P

BF = jnp.bfloat16
F32 = jnp.float32
NEG = -1e30
H_DEV = 4
ROWS = 128
NOPE = 128
ROPE = 64
KVR = 512
VD = 128
BLOCK = 64
WIDE = 640
PAIR = 1152
PARTS = 2
CHUNK = 512
QUAD = 4
COEF = float((NOPE + ROPE) ** -0.5 * np.log2(np.e))
INTERPRET = False
KEY = KVR + ROPE

SAME_HALF = [[x * 4 + z * 2 + c for x in range(4) for c in range(2)] for z in range(2)]


def nt_dot(a, b):
    return lax.dot_general(a, b, (((1,), (1,)), ((), ())), preferred_element_type=F32)


def dot(a, b):
    return jnp.dot(a, b, preferred_element_type=F32)


def pieces(x, n):
    out = []
    for _ in range(n):
        part = x.astype(BF).astype(F32)
        out.append(part)
        x = x - part
    return out


def with_stats(tops, totals, rows):
    lane = lax.broadcasted_iota(jnp.int32, (rows, 128), 1)
    tail = jnp.zeros((rows, 128), F32)
    for h in range(H_DEV):
        cols = pieces(tops[h], 3) + pieces(totals[h], 2)
        for k, col in enumerate(cols):
            tail = jnp.where(lane == 8 * h + k, col, tail)
    return tail


def stats_of(tail, h):
    t = tail[:, 8 * h : 8 * h + 8]
    top = t[:, 0:1] + (t[:, 1:2] + t[:, 2:3])
    return top, t[:, 3:4] + t[:, 4:5]


def stage(kv_ref, out_ref):
    rows = kv_ref.shape[0]
    keys = [kv_ref[:, t * PAIR : (t + 1) * PAIR][:, o : o + KEY] for t in range(QUAD) for o in (0, KEY)]
    pad = jnp.zeros((rows, WIDE - KEY), BF)
    out_ref[...] = jnp.concatenate([jnp.concatenate([k, pad], axis=1) for k in keys], axis=0)


def staged(kv):
    steps = kv.shape[1] // (PAIR * QUAD)
    chunk = kv.shape[0] * 2 * QUAD
    return pl.pallas_call(
        stage,
        grid=(steps,),
        out_shape=jax.ShapeDtypeStruct((steps * chunk, WIDE), BF),
        in_specs=[pl.BlockSpec((kv.shape[0], PAIR * QUAD), lambda i: (0, i))],
        out_specs=pl.BlockSpec((chunk, WIDE), lambda i: (i, 0)),
        compiler_params=pltpu.CompilerParams(vmem_limit_bytes=16 * 2**20),
        interpret=INTERPRET,
    )(kv)


def attend(q_ref, we_ref, vue_ref, bias_ref, k_hbm, out_ref, qe, s_ref, p_ref, k_ref, sems):
    copies = {}
    for n, first in enumerate(range(0, k_ref.shape[0], CHUNK)):
        rows = pl.ds(first, CHUNK)
        copies[first] = pltpu.make_async_copy(k_hbm.at[rows], k_ref.at[rows], sems.at[n])
        copies[first].start()
    n_part = k_ref.shape[0] // PARTS
    for h in range(H_DEV):
        start = (h // 2) * 384 + (h % 2) * 128
        qs = q_ref[:, start : start + 256]
        qe[h * ROWS : (h + 1) * ROWS, :] = dot(qs, we_ref[h]).astype(BF)
    bias = jnp.concatenate([bias_ref[...]] * H_DEV, axis=0)

    def score(first, top):
        copies[first].wait()
        s = nt_dot(qe[...], k_ref[first : first + CHUNK, :])
        for at in range(0, CHUNK, 128):
            piece = s[:, at : at + 128] + bias
            top = jnp.maximum(top, piece)
            s_ref[:, first + at : first + at + 128] = piece
        return top

    def weigh(first, top, total):
        for at in range(first, first + CHUNK, 128):
            w = jnp.exp2((s_ref[:, at : at + 128] - top) * COEF)
            total = total + w
            p_ref[:, at : at + 128] = w.astype(BF)
        return total

    lowest = jnp.full((H_DEV * ROWS, 128), NEG, F32)
    tops, totals, accs = [], [], []
    top = lowest
    for first in range(0, n_part, CHUNK):
        top = score(first, top)
    tops.append(jnp.max(top, axis=1, keepdims=True))
    for part in range(PARTS):
        begin = part * n_part
        total = jnp.zeros((H_DEV * ROWS, 128), F32)
        top = lowest
        for first in range(begin, begin + n_part, CHUNK):
            if part + 1 < PARTS:
                top = score(first + n_part, top)
            total = weigh(first, tops[part], total)
        if part + 1 < PARTS:
            tops.append(jnp.max(top, axis=1, keepdims=True))
        totals.append(jnp.sum(total, axis=1, keepdims=True))
        accs.append(dot(p_ref[:, begin : begin + n_part], k_ref[begin : begin + n_part, :KVR]))
    top = tops[0]
    for t in tops[1:]:
        top = jnp.maximum(top, t)
    acc, total = 0.0, 0.0
    for a, t, l in zip(accs, tops, totals):
        f = jnp.exp2((t - top) * COEF)
        acc = acc + f * a
        total = total + f * l
    acc = acc.astype(BF)
    heads = [slice(h * ROWS, (h + 1) * ROWS) for h in range(H_DEV)]
    for h, rows in enumerate(heads):
        out_ref[:, h * VD : (h + 1) * VD] = dot(acc[rows], vue_ref[h]).astype(BF)
    tail = with_stats([top[rows] for rows in heads], [total[rows] for rows in heads], ROWS)
    out_ref[:, H_DEV * VD :] = tail.astype(BF)


def merge(parts, tails):
    nums, tops, totals = [], [], []
    for h in range(H_DEV):
        stats = [stats_of(t, h) for t in tails]
        top = stats[0][0]
        for m, _ in stats[1:]:
            top = jnp.maximum(top, m)
        num, total = 0.0, 0.0
        for part, (m, l) in zip(parts, stats):
            f = jnp.exp2((m - top) * COEF)
            num = num + part[:, h * VD : (h + 1) * VD] * f
            total = total + l * f
        nums.append(num)
        tops.append(top)
        totals.append(total)
    return nums, tops, totals


def merge_half(in_ref, out_ref):
    n, rows, _ = in_ref.shape
    data = [in_ref[s].astype(F32) for s in range(n)]
    nums, tops, totals = merge([d[:, : H_DEV * VD] for d in data], [d[:, H_DEV * VD :] for d in data])
    whole = jnp.concatenate(nums + [with_stats(tops, totals, rows)], axis=1).astype(BF)
    for k in range(out_ref.shape[0]):
        out_ref[k] = whole


def project(in_ref, w_ref, out_ref):
    data = [
        jnp.concatenate(
            [in_ref[x * 4 + z * 2 + c].astype(F32) for x in range(4) for c in range(2)], axis=0
        )
        for z in range(2)
    ]
    nums, _, totals = merge([d[:, : H_DEV * VD] for d in data], [d[:, H_DEV * VD :] for d in data])
    value = jnp.concatenate([n / t for n, t in zip(nums, totals)], axis=1).astype(BF)
    out_ref[...] = nt_dot(value, w_ref[...]).astype(BF)


def call(kernel, out_shape, *args, scratch=(), spaces=None, limit=16):
    return pl.pallas_call(
        kernel,
        out_shape=out_shape,
        in_specs=[pl.BlockSpec(memory_space=m) for m in spaces or [pltpu.VMEM] * len(args)],
        out_specs=pl.BlockSpec(memory_space=pltpu.VMEM),
        scratch_shapes=list(scratch),
        compiler_params=pltpu.CompilerParams(vmem_limit_bytes=limit * 2**20),
        interpret=INTERPRET,
    )(*args)


def body(queries, w_uk, value_up_weight, w_out, kv_cache, blocks):
    n_ctx = lax.axis_size("ctx")
    n_blocks = kv_cache.shape[0]
    q = lax.all_to_all(jnp.broadcast_to(queries[None], (n_ctx,) + queries.shape), "ctx", 0, 0)
    q = q.reshape(ROWS, -1)

    eye = jnp.broadcast_to(jnp.eye(ROPE, dtype=BF)[None], (H_DEV, ROPE, ROPE))
    nope = jnp.pad(w_uk, ((0, 0), (0, 0), (0, WIDE - KVR)))
    rope = jnp.pad(eye, ((0, 0), (0, 0), (KVR, WIDE - KVR - ROPE)))
    both = jnp.concatenate([nope, rope], axis=1).reshape(H_DEV // 2, 2, NOPE + ROPE, WIDE)
    zero = jnp.zeros_like(both[:, 0, :ROPE])
    first = jnp.concatenate([both[:, 0], zero], axis=1)
    second = jnp.concatenate([zero, both[:, 1]], axis=1)
    absorb = jnp.stack([first, second], axis=1).reshape(H_DEV, 256, WIDE)

    offsets = blocks - lax.axis_index("ctx") * n_blocks
    lane = jnp.arange(2 * n_blocks, dtype=jnp.int32) % n_blocks
    present = jnp.any(offsets[:, :, None] == lane[None, None, :], axis=1)
    bias = jnp.where(present, 0.0, NEG).astype(F32)

    keys = pltpu.with_memory_space_constraint(staged(kv_cache), pltpu.HBM)
    parts = call(
        attend,
        jax.ShapeDtypeStruct((ROWS, WIDE), BF),
        q, absorb, value_up_weight, bias, keys,
        scratch=[
            pltpu.VMEM((H_DEV * ROWS, WIDE), BF),
            pltpu.VMEM((H_DEV * ROWS, keys.shape[0]), F32),
            pltpu.VMEM((H_DEV * ROWS, keys.shape[0]), BF),
            pltpu.VMEM(keys.shape, BF),
            pltpu.SemaphoreType.DMA((keys.shape[0] // CHUNK,)),
        ],
        spaces=[pltpu.VMEM] * 4 + [pltpu.HBM],
        limit=40,
    )
    own = ROWS // (n_ctx // 2)
    parts = lax.all_to_all(
        parts.reshape(n_ctx // 2, own, WIDE), "ctx", 0, 0, axis_index_groups=SAME_HALF
    )
    halves = call(merge_half, jax.ShapeDtypeStruct((n_ctx, own, WIDE), BF), parts)
    halves = lax.all_to_all(halves, "ctx", 0, 0)
    partial = call(project, jax.ShapeDtypeStruct((ROWS, w_out.shape[1]), BF), halves, w_out.T)
    n_head = lax.axis_size("head")
    shares = lax.all_to_all(partial.reshape(n_head, ROWS // n_head, -1), "head", 0, 0)
    return jnp.sum(shares.astype(F32), axis=0).astype(BF)


def solution(mesh):
    return jax.shard_map(
        body,
        mesh=mesh,
        in_specs=(
            P("ctx", "head"),
            P("head", None, None),
            P("head", None, None),
            P("head", "ctx"),
            P("ctx", None),
            P(),
        ),
        out_specs=P("head", "ctx"),
        check_vma=False,
    )
```

```python
import numpy as np
import jax
import jax.numpy as jnp
from jax import lax
from jax.experimental import pallas as pl
from jax.experimental.pallas import tpu as pltpu
from jax.sharding import PartitionSpec as P

BF = jnp.bfloat16
F32 = jnp.float32
NEG = -1e30
H_DEV = 4
ROWS = 128
NOPE = 128
ROPE = 64
KVR = 512
VD = 128
BLOCK = 64
WIDE = 640
PAIR = 1152
PARTS = (0.25, 0.375, 0.375)
CHUNK = 512
QUAD = 4
COEF = float((NOPE + ROPE) ** -0.5 * np.log2(np.e))
INTERPRET = False
KEY = KVR + ROPE

SAME_CORE = [[x * 4 + z * 2 + c for x in range(4) for z in range(2)] for c in range(2)]
SAME_CHIP = [[x * 4 + z * 2 + c for c in range(2)] for x in range(4) for z in range(2)]
SAME_HALF = [[x * 4 + z * 2 + c for c in range(2) for x in range(4)] for z in range(2)]


def nt_dot(a, b):
    return lax.dot_general(a, b, (((1,), (1,)), ((), ())), preferred_element_type=F32)


def dot(a, b):
    return jnp.dot(a, b, preferred_element_type=F32)


def tn_dot(a, b):
    return lax.dot_general(a, b, (((0,), (0,)), ((), ())), preferred_element_type=F32)


def pieces(x, n):
    out = []
    for _ in range(n):
        part = x.astype(BF).astype(F32)
        out.append(part)
        x = x - part
    return out


def with_stats(tops, totals, rows):
    lane = lax.broadcasted_iota(jnp.int32, (rows, 128), 1)
    tail = jnp.zeros((rows, 128), F32)
    for h in range(H_DEV):
        cols = pieces(tops[h], 3) + pieces(totals[h], 2)
        for k, col in enumerate(cols):
            tail = jnp.where(lane == 8 * h + k, col, tail)
    return tail


def stats_of(tail, h):
    t = tail[:, 8 * h : 8 * h + 8]
    top = t[:, 0:1] + (t[:, 1:2] + t[:, 2:3])
    return top, t[:, 3:4] + t[:, 4:5]


def stage(kv_ref, out_ref):
    rows = kv_ref.shape[0]
    keys = [kv_ref[:, t * PAIR : (t + 1) * PAIR][:, o : o + KEY] for t in range(QUAD) for o in (0, KEY)]
    pad = jnp.zeros((rows, WIDE - KEY), BF)
    out_ref[...] = jnp.concatenate([jnp.concatenate([k, pad], axis=1) for k in keys], axis=0)


def staged(kv):
    steps = kv.shape[1] // (PAIR * QUAD)
    chunk = kv.shape[0] * 2 * QUAD
    return pl.pallas_call(
        stage,
        grid=(steps,),
        out_shape=jax.ShapeDtypeStruct((steps * chunk, WIDE), BF),
        in_specs=[pl.BlockSpec((kv.shape[0], PAIR * QUAD), lambda i: (0, i))],
        out_specs=pl.BlockSpec((chunk, WIDE), lambda i: (i, 0)),
        compiler_params=pltpu.CompilerParams(vmem_limit_bytes=16 * 2**20),
        interpret=INTERPRET,
    )(kv)


def attend(q_ref, wt_ref, vue_ref, bias_ref, k_hbm, out_ref, qt, s_ref, p_ref, k_ref, sems):
    width = qt.shape[1]
    rows = width // H_DEV
    bounds = [0]
    for share in PARTS:
        bounds.append(bounds[-1] + int(share * k_ref.shape[0]))
    spans = list(zip(bounds, bounds[1:]))
    copies = []
    for n, (a, b) in enumerate(spans):
        span = pl.ds(a, b - a)
        copies.append(pltpu.make_async_copy(k_hbm.at[span], k_ref.at[span], sems.at[n]))
        copies[-1].start()
    for h in range(H_DEV):
        start = (h // 2) * 384 + (h % 2) * 128
        q = q_ref[:, start : start + 256]
        qt[:, h * rows : (h + 1) * rows] = nt_dot(wt_ref[h], q).astype(BF)

    def score(first, top):
        s = dot(k_ref[first : first + CHUNK, :], qt[...])
        for at in range(0, CHUNK, 128):
            piece = s[at : at + 128, :] + jnp.concatenate([bias_ref[...]] * H_DEV, axis=1)
            top = jnp.maximum(top, jnp.max(piece.reshape(16, 8, width), axis=0))
            s_ref[first + at : first + at + 128, :] = piece
        return top

    def weigh(first, top, total):
        for at in range(first, first + CHUNK, 128):
            w = jnp.exp2((s_ref[at : at + 128, :] - top) * COEF)
            total = total + jnp.sum(w.reshape(16, 8, width), axis=0)
            p_ref[at : at + 128, :] = w.astype(BF)
        return total

    lowest = jnp.full((8, width), NEG, F32)
    tops, totals, accs = [], [], []
    copies[0].wait()
    top = lowest
    for first in range(spans[0][0], spans[0][1], CHUNK):
        top = score(first, top)
    tops.append(jnp.max(top, axis=0, keepdims=True))
    for n, (a, b) in enumerate(spans):
        total = jnp.zeros((8, width), F32)
        top = lowest
        now = list(range(a, b, CHUNK))
        later = []
        if n + 1 < len(spans):
            copies[n + 1].wait()
            later = list(range(spans[n + 1][0], spans[n + 1][1], CHUNK))
        while now or later:
            if later:
                top = score(later.pop(0), top)
            if now:
                total = weigh(now.pop(0), tops[n], total)
        if n + 1 < len(spans):
            tops.append(jnp.max(top, axis=0, keepdims=True))
        totals.append(jnp.sum(total, axis=0, keepdims=True))
        accs.append(tn_dot(p_ref[a:b, :], k_ref[a:b, :KVR]))
    top = tops[0]
    for t in tops[1:]:
        top = jnp.maximum(top, t)
    acc, total = 0.0, 0.0
    for a, t, l in zip(accs, tops, totals):
        f = jnp.exp2((t - top) * COEF)
        acc = acc + a * f.reshape(width, 1)
        total = total + f * l
    acc = acc.astype(BF)
    line = lax.broadcasted_iota(jnp.int32, (128, rows), 0)
    tail = jnp.zeros((128, rows), F32)
    for h in range(H_DEV):
        own = slice(h * rows, (h + 1) * rows)
        out_ref[:, h * VD : (h + 1) * VD] = dot(acc[own], vue_ref[h]).astype(BF)
        for k, row in enumerate(pieces(top[:, own], 3) + pieces(total[:, own], 2)):
            tail = jnp.where(line == 8 * h + k, row, tail)
    out_ref[:, H_DEV * VD :] = tail.T.astype(BF)


def merge(parts, tails):
    nums, tops, totals = [], [], []
    for h in range(H_DEV):
        stats = [stats_of(t, h) for t in tails]
        top = stats[0][0]
        for m, _ in stats[1:]:
            top = jnp.maximum(top, m)
        num, total = 0.0, 0.0
        for part, (m, l) in zip(parts, stats):
            f = jnp.exp2((m - top) * COEF)
            num = num + part[:, h * VD : (h + 1) * VD] * f
            total = total + l * f
        nums.append(num)
        tops.append(top)
        totals.append(total)
    return nums, tops, totals


def merge_half(in_ref, out_ref):
    n, rows, _ = in_ref.shape
    data = [in_ref[s].astype(F32) for s in range(n)]
    nums, tops, totals = merge([d[:, : H_DEV * VD] for d in data], [d[:, H_DEV * VD :] for d in data])
    whole = jnp.concatenate(nums + [with_stats(tops, totals, rows)], axis=1).astype(BF)
    for k in range(out_ref.shape[0]):
        out_ref[k] = whole


def project(in_ref, w_ref, out_ref):
    groups = in_ref.shape[0] // 2
    data = [
        jnp.concatenate([in_ref[2 * g + z].astype(F32) for g in range(groups)], axis=0)
        for z in range(2)
    ]
    nums, _, totals = merge([d[:, : H_DEV * VD] for d in data], [d[:, H_DEV * VD :] for d in data])
    value = jnp.concatenate([n / t for n, t in zip(nums, totals)], axis=1).astype(BF)
    res = nt_dot(value, w_ref[...])
    order = [res[(c * 8 + xz) * 8 : (c * 8 + xz) * 8 + 8] for xz in range(8) for c in range(2)]
    out_ref[...] = jnp.concatenate(order, axis=0).astype(BF)


def call(kernel, out_shape, *args, scratch=(), spaces=None, limit=16):
    return pl.pallas_call(
        kernel,
        out_shape=out_shape,
        in_specs=[pl.BlockSpec(memory_space=m) for m in spaces or [pltpu.VMEM] * len(args)],
        out_specs=pl.BlockSpec(memory_space=pltpu.VMEM),
        scratch_shapes=list(scratch),
        compiler_params=pltpu.CompilerParams(vmem_limit_bytes=limit * 2**20),
        interpret=INTERPRET,
    )(*args)


def copies_to_all(copied):
    got = lax.all_to_all(copied, "ctx", 0, 0, axis_index_groups=SAME_CORE)
    return lax.all_gather(got, "ctx", axis=0, tiled=True, axis_index_groups=SAME_CHIP)


def body(queries, w_uk, value_up_weight, w_out, kv_cache, blocks):
    n_ctx = lax.axis_size("ctx")
    n_blocks = kv_cache.shape[0]
    own_rows = queries.shape[0]
    q = copies_to_all(jnp.broadcast_to(queries[None], (n_ctx // 2,) + queries.shape))
    q = q.reshape(ROWS, -1)

    eye = jnp.broadcast_to(jnp.eye(ROPE, dtype=BF)[None], (H_DEV, ROPE, ROPE))
    nope = jnp.pad(w_uk, ((0, 0), (0, 0), (0, WIDE - KVR)))
    rope = jnp.pad(eye, ((0, 0), (0, 0), (KVR, WIDE - KVR - ROPE)))
    both = jnp.concatenate([nope, rope], axis=1).reshape(H_DEV // 2, 2, NOPE + ROPE, WIDE)
    zero = jnp.zeros_like(both[:, 0, :ROPE])
    first = jnp.concatenate([both[:, 0], zero], axis=1)
    second = jnp.concatenate([zero, both[:, 1]], axis=1)
    absorb = jnp.stack([first, second], axis=1).reshape(H_DEV, 256, WIDE)

    picked = blocks.reshape(4, 2, 2, own_rows, -1).transpose(2, 0, 1, 3, 4).reshape(ROWS, -1)
    offsets = picked - lax.axis_index("ctx") * n_blocks
    key = jnp.arange(2 * n_blocks, dtype=jnp.int32) % n_blocks
    present = jnp.any(offsets.T[None, :, :] == key[:, None, None], axis=1)
    bias = jnp.where(present, 0.0, NEG).astype(F32)

    keys = pltpu.with_memory_space_constraint(staged(kv_cache), pltpu.HBM)
    width = H_DEV * ROWS
    parts = call(
        attend,
        jax.ShapeDtypeStruct((ROWS, WIDE), BF),
        q, absorb.transpose(0, 2, 1), value_up_weight, bias, keys,
        scratch=[
            pltpu.VMEM((WIDE, width), BF),
            pltpu.VMEM((keys.shape[0], width), F32),
            pltpu.VMEM((keys.shape[0], width), BF),
            pltpu.VMEM(keys.shape, BF),
            pltpu.SemaphoreType.DMA((len(PARTS),)),
        ],
        spaces=[pltpu.VMEM] * 4 + [pltpu.HBM],
        limit=40,
    )
    own = ROWS // (n_ctx // 2)
    parts = lax.all_to_all(
        parts.reshape(n_ctx // 2, own, WIDE), "ctx", 0, 0, axis_index_groups=SAME_HALF
    )
    halves = call(merge_half, jax.ShapeDtypeStruct((n_ctx // 2, own, WIDE), BF), parts)
    halves = copies_to_all(halves)
    partial = call(project, jax.ShapeDtypeStruct((ROWS, w_out.shape[1]), BF), halves, w_out.T)
    n_head = lax.axis_size("head")
    shares = lax.all_to_all(partial.reshape(n_head, ROWS // n_head, -1), "head", 0, 0)
    return jnp.sum(shares.astype(F32), axis=0).astype(BF)


def solution(mesh):
    return jax.shard_map(
        body,
        mesh=mesh,
        in_specs=(
            P("ctx", "head"),
            P("head", None, None),
            P("head", None, None),
            P("head", "ctx"),
            P("ctx", None),
            P(),
        ),
        out_specs=P("head", "ctx"),
        check_vma=False,
    )
```

```python
import numpy as np
import jax
import jax.numpy as jnp
from jax import lax
from jax.experimental import pallas as pl
from jax.experimental.pallas import tpu as pltpu
from jax.sharding import PartitionSpec as P

BF = jnp.bfloat16
F32 = jnp.float32
NEG = -1e30
H_DEV = 4
ROWS = 128
NOPE = 128
ROPE = 64
KVR = 512
VD = 128
BLOCK = 64
WIDE = 640
PAIR = 1152
PARTS = (0.25, 0.375, 0.375)
CHUNK = 512
QUAD = 4
COEF = float((NOPE + ROPE) ** -0.5 * np.log2(np.e))
INTERPRET = False
KEY = KVR + ROPE

SAME_CORE = [[x * 4 + z * 2 + c for x in range(4) for z in range(2)] for c in range(2)]
SAME_CHIP = [[x * 4 + z * 2 + c for c in range(2)] for x in range(4) for z in range(2)]
SAME_HALF = [[x * 4 + z * 2 + c for c in range(2) for x in range(4)] for z in range(2)]


def nt_dot(a, b):
    return lax.dot_general(a, b, (((1,), (1,)), ((), ())), preferred_element_type=F32)


def dot(a, b):
    return jnp.dot(a, b, preferred_element_type=F32)


def tn_dot(a, b):
    return lax.dot_general(a, b, (((0,), (0,)), ((), ())), preferred_element_type=F32)


def pieces(x, n):
    out = []
    for _ in range(n):
        part = x.astype(BF).astype(F32)
        out.append(part)
        x = x - part
    return out


def with_stats(tops, totals, rows):
    lane = lax.broadcasted_iota(jnp.int32, (rows, 128), 1)
    tail = jnp.zeros((rows, 128), F32)
    for h in range(H_DEV):
        cols = pieces(tops[h], 3) + pieces(totals[h], 2)
        for k, col in enumerate(cols):
            tail = jnp.where(lane == 8 * h + k, col, tail)
    return tail


def stats_of(tail, h):
    t = tail[:, 8 * h : 8 * h + 8]
    top = t[:, 0:1] + (t[:, 1:2] + t[:, 2:3])
    return top, t[:, 3:4] + t[:, 4:5]


def in_hbm(x):
    return pltpu.with_memory_space_constraint(x, pltpu.HBM)


def stage(kv_ref, blocks_ref, shard_ref, out_ref, bias_ref):
    count = kv_ref.shape[0]
    keys = [kv_ref[:, t * PAIR : (t + 1) * PAIR][:, o : o + KEY] for t in range(QUAD) for o in (0, KEY)]
    pad = jnp.zeros((count, WIDE - KEY), BF)
    out_ref[...] = jnp.concatenate([jnp.concatenate([k, pad], axis=1) for k in keys], axis=0)

    @pl.when(pl.program_id(0) == 0)
    def _():
        b = blocks_ref[...]
        n = ROWS // 16
        order = [xz * 2 + c for c in range(2) for xz in range(8)]
        b = jnp.concatenate([b[:, k * n : (k + 1) * n] for k in order], axis=1)
        b = b - shard_ref[0] * count
        line = lax.broadcasted_iota(jnp.int32, (count, ROWS), 0)
        bias = jnp.full((count, ROWS), NEG, F32)
        for k in range(b.shape[0]):
            bias = jnp.where(b[k : k + 1, :] == line, 0.0, bias)
        bias_ref[...] = jnp.concatenate([bias, bias], axis=0)


def staged(kv, blocks, shard):
    steps = kv.shape[1] // (PAIR * QUAD)
    chunk = kv.shape[0] * 2 * QUAD
    return pl.pallas_call(
        stage,
        grid=(steps,),
        out_shape=(
            pltpu.HBM((steps * chunk, WIDE), BF),
            jax.ShapeDtypeStruct((2 * kv.shape[0], ROWS), F32),
        ),
        in_specs=[
            pl.BlockSpec((kv.shape[0], PAIR * QUAD), lambda i: (0, i)),
            pl.BlockSpec(blocks.shape, lambda i: (0, 0)),
            pl.BlockSpec(memory_space=pltpu.SMEM),
        ],
        out_specs=(
            pl.BlockSpec((chunk, WIDE), lambda i: (i, 0)),
            pl.BlockSpec((2 * kv.shape[0], ROWS), lambda i: (0, 0)),
        ),
        compiler_params=pltpu.CompilerParams(vmem_limit_bytes=16 * 2**20),
        interpret=INTERPRET,
    )(in_hbm(kv), blocks, shard)


def attend(q_ref, w_ref, vue_ref, bias_ref, k_hbm, out_ref, qt, s_ref, p_ref, k_ref, sems):
    width = qt.shape[1]
    rows = width // H_DEV
    bounds = [0]
    for share in PARTS:
        bounds.append(bounds[-1] + int(share * k_ref.shape[0]))
    spans = list(zip(bounds, bounds[1:]))
    copies = []
    for n, (a, b) in enumerate(spans):
        span = pl.ds(a, b - a)
        copies.append(pltpu.make_async_copy(k_hbm.at[span], k_ref.at[span], sems.at[n]))
        copies[-1].start()
    qt[KEY:, :] = jnp.zeros((WIDE - KEY, width), BF)
    for h in range(H_DEV):
        own = slice(h * rows, (h + 1) * rows)
        q = q_ref[:, h * (NOPE + ROPE) : (h + 1) * (NOPE + ROPE)]
        absorbed = lax.dot_general(
            w_ref[h], q[:, :NOPE], (((0,), (1,)), ((), ())), preferred_element_type=F32
        )
        qt[:KVR, own] = absorbed.astype(BF)
        qt[KVR:KEY, own] = q[:, NOPE:].T

    def score(first, top):
        s = dot(k_ref[first : first + CHUNK, :], qt[...])
        for at in range(0, CHUNK, 128):
            piece = s[at : at + 128, :] + jnp.concatenate([bias_ref[...]] * H_DEV, axis=1)
            top = jnp.maximum(top, jnp.max(piece.reshape(16, 8, width), axis=0))
            s_ref[first + at : first + at + 128, :] = piece
        return top

    def weigh(first, top, total):
        for at in range(first, first + CHUNK, 128):
            w = jnp.exp2((s_ref[at : at + 128, :] - top) * COEF)
            total = total + jnp.sum(w.reshape(16, 8, width), axis=0)
            p_ref[at : at + 128, :] = w.astype(BF)
        return total

    lowest = jnp.full((8, width), NEG, F32)
    tops, totals, accs = [], [], []
    copies[0].wait()
    top = lowest
    for first in range(spans[0][0], spans[0][1], CHUNK):
        top = score(first, top)
    tops.append(jnp.max(top, axis=0, keepdims=True))
    for n, (a, b) in enumerate(spans):
        total = jnp.zeros((8, width), F32)
        top = lowest
        now = list(range(a, b, CHUNK))
        later = []
        if n + 1 < len(spans):
            copies[n + 1].wait()
            later = list(range(spans[n + 1][0], spans[n + 1][1], CHUNK))
        while now or later:
            if later:
                top = score(later.pop(0), top)
            if now:
                total = weigh(now.pop(0), tops[n], total)
        if n + 1 < len(spans):
            tops.append(jnp.max(top, axis=0, keepdims=True))
        totals.append(jnp.sum(total, axis=0, keepdims=True))
        accs.append(tn_dot(p_ref[a:b, :], k_ref[a:b, :KVR]))
    top = tops[0]
    for t in tops[1:]:
        top = jnp.maximum(top, t)
    acc, total = 0.0, 0.0
    for a, t, l in zip(accs, tops, totals):
        f = jnp.exp2((t - top) * COEF)
        acc = acc + a * f.reshape(width, 1)
        total = total + f * l
    acc = acc.astype(BF)
    line = lax.broadcasted_iota(jnp.int32, (128, rows), 0)
    tail = jnp.zeros((128, rows), F32)
    for h in range(H_DEV):
        own = slice(h * rows, (h + 1) * rows)
        out_ref[:, h * VD : (h + 1) * VD] = dot(acc[own], vue_ref[h]).astype(BF)
        for k, row in enumerate(pieces(top[:, own], 3) + pieces(total[:, own], 2)):
            tail = jnp.where(line == 8 * h + k, row, tail)
    out_ref[:, H_DEV * VD :] = tail.T.astype(BF)


def merge(parts, tails):
    nums, tops, totals = [], [], []
    for h in range(H_DEV):
        stats = [stats_of(t, h) for t in tails]
        top = stats[0][0]
        for m, _ in stats[1:]:
            top = jnp.maximum(top, m)
        num, total = 0.0, 0.0
        for part, (m, l) in zip(parts, stats):
            f = jnp.exp2((m - top) * COEF)
            num = num + part[:, h * VD : (h + 1) * VD] * f
            total = total + l * f
        nums.append(num)
        tops.append(top)
        totals.append(total)
    return nums, tops, totals


def merge_half(in_ref, out_ref):
    n, rows, _ = in_ref.shape
    data = [in_ref[s].astype(F32) for s in range(n)]
    nums, tops, totals = merge([d[:, : H_DEV * VD] for d in data], [d[:, H_DEV * VD :] for d in data])
    out_ref[...] = jnp.concatenate(nums + [with_stats(tops, totals, rows)], axis=1).astype(BF)


def merge_all(own_ref, other_ref, out_ref):
    data = [own_ref[...].astype(F32), other_ref[...].astype(F32)]
    nums, _, totals = merge([d[:, : H_DEV * VD] for d in data], [d[:, H_DEV * VD :] for d in data])
    value = jnp.concatenate([n / t for n, t in zip(nums, totals)], axis=1).astype(BF)
    for k in range(out_ref.shape[0]):
        out_ref[k] = value


def project(value_ref, w_ref, out_ref):
    res = nt_dot(value_ref[...], w_ref[...])
    order = [res[(c * 8 + xz) * 8 : (c * 8 + xz) * 8 + 8] for xz in range(8) for c in range(2)]
    out_ref[...] = jnp.concatenate(order, axis=0).astype(BF)


def call(kernel, out_shape, *args, scratch=(), spaces=None, limit=16):
    return pl.pallas_call(
        kernel,
        out_shape=out_shape,
        in_specs=[pl.BlockSpec(memory_space=m) for m in spaces or [pltpu.VMEM] * len(args)],
        out_specs=pl.BlockSpec(memory_space=pltpu.VMEM),
        scratch_shapes=list(scratch),
        compiler_params=pltpu.CompilerParams(vmem_limit_bytes=limit * 2**20),
        interpret=INTERPRET,
    )(*args)


def body(queries, w_uk, value_up_weight, w_out, kv_cache, blocks):
    n_ctx = lax.axis_size("ctx")
    q = jnp.broadcast_to(queries[None], (n_ctx // 2,) + queries.shape)
    q = lax.all_to_all(q, "ctx", 0, 0, axis_index_groups=SAME_CORE)
    q = lax.all_gather(q, "ctx", axis=0, tiled=True, axis_index_groups=SAME_CHIP)
    q = q.reshape(ROWS, -1)
    keys, bias = staged(kv_cache, blocks.T, lax.axis_index("ctx").reshape(1))
    width = H_DEV * ROWS
    parts = call(
        attend,
        jax.ShapeDtypeStruct((ROWS, WIDE), BF),
        q, w_uk, value_up_weight, bias, in_hbm(keys),
        scratch=[
            pltpu.VMEM((WIDE, width), BF),
            pltpu.VMEM((keys.shape[0], width), F32),
            pltpu.VMEM((keys.shape[0], width), BF),
            pltpu.VMEM(keys.shape, BF),
            pltpu.SemaphoreType.DMA((len(PARTS),)),
        ],
        spaces=[pltpu.VMEM] * 4 + [pltpu.HBM],
        limit=40,
    )
    own = ROWS // (n_ctx // 2)
    parts = lax.all_to_all(
        parts.reshape(n_ctx // 2, own, WIDE), "ctx", 0, 0, axis_index_groups=SAME_HALF
    )
    half = call(merge_half, jax.ShapeDtypeStruct((own, WIDE), BF), parts)
    other = lax.ppermute(half, "ctx", [(i, i ^ 2) for i in range(n_ctx)])
    value = call(merge_all, jax.ShapeDtypeStruct((n_ctx // 2, own, H_DEV * VD), BF), half, other)
    value = lax.all_to_all(value, "ctx", 0, 0, axis_index_groups=SAME_HALF).reshape(ROWS, -1)
    partial = call(project, jax.ShapeDtypeStruct((ROWS, w_out.shape[1]), BF), value, w_out.T)
    n_head = lax.axis_size("head")
    shares = lax.all_to_all(partial.reshape(n_head, ROWS // n_head, -1), "head", 0, 0)
    return jnp.sum(shares.astype(F32), axis=0).astype(BF)


def solution(mesh):
    return jax.shard_map(
        body,
        mesh=mesh,
        in_specs=(
            P("ctx", "head"),
            P("head", None, None),
            P("head", None, None),
            P("head", "ctx"),
            P("ctx", None),
            P(),
        ),
        out_specs=P("head", "ctx"),
        check_vma=False,
    )
```

```python
import numpy as np
import jax
import jax.numpy as jnp
from jax import lax
from jax.experimental import pallas as pl
from jax.experimental.pallas import tpu as pltpu
from jax.sharding import PartitionSpec as P

BF = jnp.bfloat16
F32 = jnp.float32
NEG = -1e30
H_DEV = 4
ROWS = 128
NOPE = 128
ROPE = 64
KVR = 512
VD = 128
BLOCK = 64
WIDE = 640
PAIR = 1152
PARTS = (0.125, 0.25, 0.3125, 0.3125)
CHUNK = 256
STAGE_PAIRS = 4
COEF = float((NOPE + ROPE) ** -0.5 * np.log2(np.e))
INTERPRET = False
KEY = KVR + ROPE

SAME_CORE = [[x * 4 + z * 2 + c for x in range(4) for z in range(2)] for c in range(2)]
SAME_CHIP = [[x * 4 + z * 2 + c for c in range(2)] for x in range(4) for z in range(2)]
SAME_HALF = [[x * 4 + z * 2 + c for c in range(2) for x in range(4)] for z in range(2)]


def nt_dot(a, b):
    return lax.dot_general(a, b, (((1,), (1,)), ((), ())), preferred_element_type=F32)


def dot(a, b):
    return jnp.dot(a, b, preferred_element_type=F32)


def tn_dot(a, b):
    return lax.dot_general(a, b, (((0,), (0,)), ((), ())), preferred_element_type=F32)


def pieces(x, n):
    out = []
    for _ in range(n):
        part = x.astype(BF).astype(F32)
        out.append(part)
        x = x - part
    return out


def with_stats(tops, totals, rows):
    lane = lax.broadcasted_iota(jnp.int32, (rows, 128), 1)
    tail = jnp.zeros((rows, 128), F32)
    for h in range(H_DEV):
        cols = pieces(tops[h], 3) + pieces(totals[h], 2)
        for k, col in enumerate(cols):
            tail = jnp.where(lane == 8 * h + k, col, tail)
    return tail


def stats_of(tail, h):
    t = tail[:, 8 * h : 8 * h + 8]
    top = t[:, 0:1] + (t[:, 1:2] + t[:, 2:3])
    return top, t[:, 3:4] + t[:, 4:5]


def in_hbm(x):
    return pltpu.with_memory_space_constraint(x, pltpu.HBM)


def stage(kv_hbm, blocks_hbm, shard_ref, out_hbm, bias_ref, kv_ref, blocks_ref, keys_ref, sems, sent):
    count, lanes = kv_ref.shape
    span = STAGE_PAIRS * PAIR
    chunk = STAGE_PAIRS * 2 * count
    steps = lanes // span
    got = []
    for i in range(steps):
        at = pl.ds(i * span, span)
        got.append(pltpu.make_async_copy(kv_hbm.at[:, at], kv_ref.at[:, at], sems.at[i]))
        got[-1].start()
    table = pltpu.make_async_copy(blocks_hbm, blocks_ref, sems.at[steps])
    table.start()
    pad = jnp.zeros((count, WIDE - KEY), BF)
    put = []
    for i in range(steps):
        got[i].wait()
        for t in range(STAGE_PAIRS):
            pair = kv_ref[:, i * span + t * PAIR : i * span + (t + 1) * PAIR]
            for o in range(2):
                key = jnp.concatenate([pair[:, o * KEY : (o + 1) * KEY], pad], axis=1)
                first = i * chunk + (2 * t + o) * count
                keys_ref[first : first + count, :] = key
        at = pl.ds(i * chunk, chunk)
        put.append(pltpu.make_async_copy(keys_ref.at[at], out_hbm.at[at], sent.at[i]))
        put[-1].start()
    table.wait()
    b = blocks_ref[...]
    n = ROWS // 16
    order = [xz * 2 + c for c in range(2) for xz in range(8)]
    b = jnp.concatenate([b[:, k * n : (k + 1) * n] for k in order], axis=1)
    b = b - shard_ref[0] * count
    line = lax.broadcasted_iota(jnp.int32, (count, ROWS), 0)
    bias = jnp.full((count, ROWS), NEG, F32)
    for k in range(b.shape[0]):
        bias = jnp.where(b[k : k + 1, :] == line, 0.0, bias)
    bias_ref[...] = jnp.concatenate([bias, bias], axis=0)
    for copy in put:
        copy.wait()


def staged(kv, blocks, shard):
    steps = kv.shape[1] // (PAIR * STAGE_PAIRS)
    keys = (kv.shape[0] * kv.shape[1] // KEY, WIDE)
    return pl.pallas_call(
        stage,
        out_shape=(pltpu.HBM(keys, BF), jax.ShapeDtypeStruct((2 * kv.shape[0], ROWS), F32)),
        in_specs=[
            pl.BlockSpec(memory_space=pltpu.HBM),
            pl.BlockSpec(memory_space=pltpu.HBM),
            pl.BlockSpec(memory_space=pltpu.SMEM),
        ],
        out_specs=(pl.BlockSpec(memory_space=pltpu.HBM), pl.BlockSpec(memory_space=pltpu.VMEM)),
        scratch_shapes=[
            pltpu.VMEM(kv.shape, BF),
            pltpu.VMEM(blocks.shape, jnp.int32),
            pltpu.VMEM(keys, BF),
            pltpu.SemaphoreType.DMA((steps + 1,)),
            pltpu.SemaphoreType.DMA((steps,)),
        ],
        compiler_params=pltpu.CompilerParams(vmem_limit_bytes=24 * 2**20),
        interpret=INTERPRET,
    )(in_hbm(kv), in_hbm(blocks), shard)


def attend(q_ref, w_ref, vue_ref, bias_ref, k_hbm, out_ref, qt, s_ref, p_ref, k_ref, sems):
    width = qt.shape[1]
    rows = width // H_DEV
    bounds = [0]
    for share in PARTS:
        bounds.append(bounds[-1] + int(share * k_ref.shape[0]))
    spans = list(zip(bounds, bounds[1:]))
    copies = []
    for n, (a, b) in enumerate(spans):
        span = pl.ds(a, b - a)
        copies.append(pltpu.make_async_copy(k_hbm.at[span], k_ref.at[span], sems.at[n]))
        copies[-1].start()
    qt[KEY:, :] = jnp.zeros((WIDE - KEY, width), BF)
    for h in range(H_DEV):
        own = slice(h * rows, (h + 1) * rows)
        q = q_ref[:, h * (NOPE + ROPE) : (h + 1) * (NOPE + ROPE)]
        absorbed = lax.dot_general(
            w_ref[h], q[:, :NOPE], (((0,), (1,)), ((), ())), preferred_element_type=F32
        )
        qt[:KVR, own] = absorbed.astype(BF)
        qt[KVR:KEY, own] = q[:, NOPE:].T

    def score(first, top):
        s = dot(k_ref[first : first + CHUNK, :], qt[...])
        for at in range(0, CHUNK, 128):
            piece = s[at : at + 128, :] + jnp.concatenate([bias_ref[...]] * H_DEV, axis=1)
            top = jnp.maximum(top, jnp.max(piece.reshape(16, 8, width), axis=0))
            s_ref[first + at : first + at + 128, :] = piece
        return top

    def weigh(first, top, total):
        for at in range(first, first + CHUNK, 128):
            w = jnp.exp2((s_ref[at : at + 128, :] - top) * COEF)
            total = total + jnp.sum(w.reshape(16, 8, width), axis=0)
            p_ref[at : at + 128, :] = w.astype(BF)
        return total

    lowest = jnp.full((8, width), NEG, F32)
    tops, totals, accs = [], [], []
    copies[0].wait()
    top = lowest
    for first in range(spans[0][0], spans[0][1], CHUNK):
        top = score(first, top)
    tops.append(jnp.max(top, axis=0, keepdims=True))
    for n, (a, b) in enumerate(spans):
        total = jnp.zeros((8, width), F32)
        top = lowest
        now = list(range(a, b, CHUNK))
        later = []
        if n + 1 < len(spans):
            copies[n + 1].wait()
            later = list(range(spans[n + 1][0], spans[n + 1][1], CHUNK))
        while now or later:
            if later:
                top = score(later.pop(0), top)
            if now:
                total = weigh(now.pop(0), tops[n], total)
        if n + 1 < len(spans):
            tops.append(jnp.max(top, axis=0, keepdims=True))
        totals.append(jnp.sum(total, axis=0, keepdims=True))
        accs.append(tn_dot(p_ref[a:b, :], k_ref[a:b, :KVR]))
    top = tops[0]
    for t in tops[1:]:
        top = jnp.maximum(top, t)
    acc, total = 0.0, 0.0
    for a, t, l in zip(accs, tops, totals):
        f = jnp.exp2((t - top) * COEF)
        acc = acc + a * f.reshape(width, 1)
        total = total + f * l
    acc = acc.astype(BF)
    line = lax.broadcasted_iota(jnp.int32, (128, rows), 0)
    tail = jnp.zeros((128, rows), F32)
    for h in range(H_DEV):
        own = slice(h * rows, (h + 1) * rows)
        out_ref[:, h * VD : (h + 1) * VD] = dot(acc[own], vue_ref[h]).astype(BF)
        for k, row in enumerate(pieces(top[:, own], 3) + pieces(total[:, own], 2)):
            tail = jnp.where(line == 8 * h + k, row, tail)
    out_ref[:, H_DEV * VD :] = tail.T.astype(BF)


def merge(parts, tails):
    nums, tops, totals = [], [], []
    for h in range(H_DEV):
        stats = [stats_of(t, h) for t in tails]
        top = stats[0][0]
        for m, _ in stats[1:]:
            top = jnp.maximum(top, m)
        num, total = 0.0, 0.0
        for part, (m, l) in zip(parts, stats):
            f = jnp.exp2((m - top) * COEF)
            num = num + part[:, h * VD : (h + 1) * VD] * f
            total = total + l * f
        nums.append(num)
        tops.append(top)
        totals.append(total)
    return nums, tops, totals


def merge_half(in_ref, out_ref):
    n, rows, _ = in_ref.shape
    data = [in_ref[s].astype(F32) for s in range(n)]
    nums, tops, totals = merge([d[:, : H_DEV * VD] for d in data], [d[:, H_DEV * VD :] for d in data])
    out_ref[...] = jnp.concatenate(nums + [with_stats(tops, totals, rows)], axis=1).astype(BF)


def merge_all(own_ref, other_ref, out_ref):
    data = [own_ref[...].astype(F32), other_ref[...].astype(F32)]
    nums, _, totals = merge([d[:, : H_DEV * VD] for d in data], [d[:, H_DEV * VD :] for d in data])
    value = jnp.concatenate([n / t for n, t in zip(nums, totals)], axis=1).astype(BF)
    for k in range(out_ref.shape[0]):
        out_ref[k] = value


def project(value_ref, w_ref, out_ref):
    res = nt_dot(value_ref[...], w_ref[...])
    order = [res[(c * 8 + xz) * 8 : (c * 8 + xz) * 8 + 8] for xz in range(8) for c in range(2)]
    out_ref[...] = jnp.concatenate(order, axis=0).astype(BF)


def call(kernel, out_shape, *args, scratch=(), spaces=None, limit=16):
    return pl.pallas_call(
        kernel,
        out_shape=out_shape,
        in_specs=[pl.BlockSpec(memory_space=m) for m in spaces or [pltpu.VMEM] * len(args)],
        out_specs=pl.BlockSpec(memory_space=pltpu.VMEM),
        scratch_shapes=list(scratch),
        compiler_params=pltpu.CompilerParams(vmem_limit_bytes=limit * 2**20),
        interpret=INTERPRET,
    )(*args)


def body(queries, w_uk, value_up_weight, w_out, kv_cache, blocks):
    n_ctx = lax.axis_size("ctx")
    q = jnp.broadcast_to(queries[None], (n_ctx // 2,) + queries.shape)
    q = lax.all_to_all(q, "ctx", 0, 0, axis_index_groups=SAME_CORE)
    q = lax.all_gather(q, "ctx", axis=0, tiled=True, axis_index_groups=SAME_CHIP)
    q = q.reshape(ROWS, -1)
    keys, bias = staged(kv_cache, blocks.T, lax.axis_index("ctx").reshape(1))
    width = H_DEV * ROWS
    parts = call(
        attend,
        jax.ShapeDtypeStruct((ROWS, WIDE), BF),
        q, w_uk, value_up_weight, bias, in_hbm(keys),
        scratch=[
            pltpu.VMEM((WIDE, width), BF),
            pltpu.VMEM((keys.shape[0], width), F32),
            pltpu.VMEM((keys.shape[0], width), BF),
            pltpu.VMEM(keys.shape, BF),
            pltpu.SemaphoreType.DMA((len(PARTS),)),
        ],
        spaces=[pltpu.VMEM] * 4 + [pltpu.HBM],
        limit=40,
    )
    own = ROWS // (n_ctx // 2)
    parts = lax.all_to_all(
        parts.reshape(n_ctx // 2, own, WIDE), "ctx", 0, 0, axis_index_groups=SAME_HALF
    )
    half = call(merge_half, jax.ShapeDtypeStruct((own, WIDE), BF), parts)
    other = lax.ppermute(half, "ctx", [(i, i ^ 2) for i in range(n_ctx)])
    value = call(merge_all, jax.ShapeDtypeStruct((n_ctx // 2, own, H_DEV * VD), BF), half, other)
    value = lax.all_to_all(value, "ctx", 0, 0, axis_index_groups=SAME_HALF).reshape(ROWS, -1)
    partial = call(project, jax.ShapeDtypeStruct((ROWS, w_out.shape[1]), BF), value, w_out.T)
    n_head = lax.axis_size("head")
    shares = lax.all_to_all(partial.reshape(n_head, ROWS // n_head, -1), "head", 0, 0)
    return jnp.sum(shares.astype(F32), axis=0).astype(BF)


def solution(mesh):
    return jax.shard_map(
        body,
        mesh=mesh,
        in_specs=(
            P("ctx", "head"),
            P("head", None, None),
            P("head", None, None),
            P("head", "ctx"),
            P("ctx", None),
            P(),
        ),
        out_specs=P("head", "ctx"),
        check_vma=False,
    )
```

```python
import numpy as np
import jax
import jax.numpy as jnp
from jax import lax
from jax.experimental import pallas as pl
from jax.experimental.pallas import tpu as pltpu
from jax.sharding import PartitionSpec as P

BF = jnp.bfloat16
F32 = jnp.float32
NEG = -1e30
H_DEV = 4
ROWS = 128
NOPE = 128
ROPE = 64
KVR = 512
VD = 128
BLOCK = 64
WIDE = 640
PAIR = 1152
PARTS = (0.125, 0.25, 0.3125, 0.3125)
CHUNK = 256
STAGE_PAIRS = 4
COEF = float((NOPE + ROPE) ** -0.5 * np.log2(np.e))
INTERPRET = False
KEY = KVR + ROPE

SAME_HALF = [[x * 4 + z * 2 + c for c in range(2) for x in range(4)] for z in range(2)]
OTHER_HALF = [(i, i ^ 2) for i in range(16)]


def nt_dot(a, b):
    return lax.dot_general(a, b, (((1,), (1,)), ((), ())), preferred_element_type=F32)


def dot(a, b):
    return jnp.dot(a, b, preferred_element_type=F32)


def tn_dot(a, b):
    return lax.dot_general(a, b, (((0,), (0,)), ((), ())), preferred_element_type=F32)


def pieces(x, n):
    out = []
    for _ in range(n):
        part = x.astype(BF).astype(F32)
        out.append(part)
        x = x - part
    return out


def with_stats(tops, totals, rows):
    lane = lax.broadcasted_iota(jnp.int32, (rows, 128), 1)
    tail = jnp.zeros((rows, 128), F32)
    for h in range(H_DEV):
        cols = pieces(tops[h], 3) + pieces(totals[h], 2)
        for k, col in enumerate(cols):
            tail = jnp.where(lane == 8 * h + k, col, tail)
    return tail


def stats_of(tail, h):
    t = tail[:, 8 * h : 8 * h + 8]
    top = t[:, 0:1] + (t[:, 1:2] + t[:, 2:3])
    return top, t[:, 3:4] + t[:, 4:5]


def in_hbm(x):
    return pltpu.with_memory_space_constraint(x, pltpu.HBM)


def stage(
    kv_hbm, blocks_hbm, shard_ref, out_hbm, near_ref, far_ref, kv_ref, blocks_ref, keys_ref, sems, sent
):
    count, lanes = kv_ref.shape
    span = STAGE_PAIRS * PAIR
    chunk = STAGE_PAIRS * 2 * count
    steps = lanes // span
    got = []
    for i in range(steps):
        at = pl.ds(i * span, span)
        got.append(pltpu.make_async_copy(kv_hbm.at[:, at], kv_ref.at[:, at], sems.at[i]))
        got[-1].start()
    table = pltpu.make_async_copy(blocks_hbm, blocks_ref, sems.at[steps])
    table.start()
    pad = jnp.zeros((count, WIDE - KEY), BF)
    put = []
    for i in range(steps):
        got[i].wait()
        for t in range(STAGE_PAIRS):
            pair = kv_ref[:, i * span + t * PAIR : i * span + (t + 1) * PAIR]
            for o in range(2):
                key = jnp.concatenate([pair[:, o * KEY : (o + 1) * KEY], pad], axis=1)
                first = i * chunk + (2 * t + o) * count
                keys_ref[first : first + count, :] = key
        at = pl.ds(i * chunk, chunk)
        put.append(pltpu.make_async_copy(keys_ref.at[at], out_hbm.at[at], sent.at[i]))
        put[-1].start()
    table.wait()
    b = blocks_ref[...]
    n = ROWS // 16
    order = [x * 4 + z * 2 + c for z in range(2) for c in range(2) for x in range(4)]
    b = jnp.concatenate([b[:, k * n : (k + 1) * n] for k in order], axis=1)
    b = b - shard_ref[0] * count
    line = lax.broadcasted_iota(jnp.int32, (count, ROWS), 0)
    bias = jnp.full((count, ROWS), NEG, F32)
    for k in range(b.shape[0]):
        bias = jnp.where(b[k : k + 1, :] == line, 0.0, bias)
    halves = [
        jnp.concatenate([jnp.concatenate([part] * H_DEV, axis=1)] * 2, axis=0)
        for part in (bias[:, : ROWS // 2], bias[:, ROWS // 2 :])
    ]
    lower = shard_ref[1] == 0
    near_ref[...] = jnp.where(lower, halves[0], halves[1])
    far_ref[...] = jnp.where(lower, halves[1], halves[0])
    for copy in put:
        copy.wait()


def staged(kv, blocks, shard):
    steps = kv.shape[1] // (PAIR * STAGE_PAIRS)
    keys = (kv.shape[0] * kv.shape[1] // KEY, WIDE)
    bias = jax.ShapeDtypeStruct((2 * kv.shape[0], H_DEV * ROWS // 2), F32)
    return pl.pallas_call(
        stage,
        out_shape=(pltpu.HBM(keys, BF), bias, bias),
        in_specs=[
            pl.BlockSpec(memory_space=pltpu.HBM),
            pl.BlockSpec(memory_space=pltpu.HBM),
            pl.BlockSpec(memory_space=pltpu.SMEM),
        ],
        out_specs=(
            pl.BlockSpec(memory_space=pltpu.HBM),
            pl.BlockSpec(memory_space=pltpu.VMEM),
            pl.BlockSpec(memory_space=pltpu.VMEM),
        ),
        scratch_shapes=[
            pltpu.VMEM(kv.shape, BF),
            pltpu.VMEM(blocks.shape, jnp.int32),
            pltpu.VMEM(keys, BF),
            pltpu.SemaphoreType.DMA((steps + 1,)),
            pltpu.SemaphoreType.DMA((steps,)),
        ],
        compiler_params=pltpu.CompilerParams(vmem_limit_bytes=24 * 2**20),
        interpret=INTERPRET,
    )(in_hbm(kv), in_hbm(blocks), shard)


def attend_near(q_ref, w_ref, vue_ref, bias_ref, k_hbm, out_ref, *scratch):
    out_ref[...] = attend(q_ref, w_ref, vue_ref, bias_ref, k_hbm, *scratch).astype(BF)


def attend_far(q_ref, w_ref, vue_ref, bias_ref, near_ref, k_hbm, out_ref, *scratch):
    far = attend(q_ref, w_ref, vue_ref, bias_ref, k_hbm, *scratch)
    near = near_ref[...].astype(F32)
    for k in range(out_ref.shape[0]):
        rows = slice(k * 8, (k + 1) * 8)
        out_ref[k] = jnp.concatenate([near[rows], far[rows]], axis=0).astype(BF)


def attend(q_ref, w_ref, vue_ref, bias_ref, k_hbm, qt, s_ref, p_ref, k_ref, sems):
    width = qt.shape[1]
    rows = width // H_DEV
    bounds = [0]
    for share in PARTS:
        bounds.append(bounds[-1] + int(share * k_ref.shape[0]))
    spans = list(zip(bounds, bounds[1:]))
    copies = []
    for n, (a, b) in enumerate(spans):
        span = pl.ds(a, b - a)
        copies.append(pltpu.make_async_copy(k_hbm.at[span], k_ref.at[span], sems.at[n]))
        copies[-1].start()
    columns = []
    for h in range(H_DEV):
        q = q_ref[:, h * (NOPE + ROPE) : (h + 1) * (NOPE + ROPE)]
        absorbed = lax.dot_general(
            w_ref[h], q[:, :NOPE], (((0,), (1,)), ((), ())), preferred_element_type=F32
        )
        columns.append((absorbed, q[:, NOPE:].astype(F32).T))
    qt[:KVR, :] = jnp.concatenate([a for a, _ in columns], axis=1).astype(BF)
    qt[KVR:KEY, :] = jnp.concatenate([r for _, r in columns], axis=1).astype(BF)
    qt[KEY:, :] = jnp.zeros((WIDE - KEY, width), BF)

    def score(first, top):
        s = dot(k_ref[first : first + CHUNK, :], qt[...])
        for at in range(0, CHUNK, 128):
            piece = s[at : at + 128, :] + bias_ref[...]
            top = jnp.maximum(top, jnp.max(piece.reshape(16, 8, width), axis=0))
            s_ref[first + at : first + at + 128, :] = piece
        return top

    def weigh(first, top, total):
        for at in range(first, first + CHUNK, 128):
            w = jnp.exp2((s_ref[at : at + 128, :] - top) * COEF)
            total = total + jnp.sum(w.reshape(16, 8, width), axis=0)
            p_ref[at : at + 128, :] = w.astype(BF)
        return total

    lowest = jnp.full((8, width), NEG, F32)
    tops, totals, accs = [], [], []
    copies[0].wait()
    top = lowest
    for first in range(spans[0][0], spans[0][1], CHUNK):
        top = score(first, top)
    tops.append(jnp.max(top, axis=0, keepdims=True))
    for n, (a, b) in enumerate(spans):
        total = jnp.zeros((8, width), F32)
        top = lowest
        now = list(range(a, b, CHUNK))
        later = []
        if n + 1 < len(spans):
            copies[n + 1].wait()
            later = list(range(spans[n + 1][0], spans[n + 1][1], CHUNK))
        while now or later:
            if later:
                top = score(later.pop(0), top)
            if now:
                total = weigh(now.pop(0), tops[n], total)
        if n + 1 < len(spans):
            tops.append(jnp.max(top, axis=0, keepdims=True))
        totals.append(jnp.sum(total, axis=0, keepdims=True))
        accs.append(tn_dot(p_ref[a:b, :], k_ref[a:b, :KVR]))
    top = tops[0]
    for t in tops[1:]:
        top = jnp.maximum(top, t)
    acc, total = 0.0, 0.0
    for a, t, l in zip(accs, tops, totals):
        f = jnp.exp2((t - top) * COEF)
        acc = acc + a * f.reshape(width, 1)
        total = total + f * l
    acc = acc.astype(BF)
    line = lax.broadcasted_iota(jnp.int32, (128, rows), 0)
    tail = jnp.zeros((128, rows), F32)
    values = []
    for h in range(H_DEV):
        own = slice(h * rows, (h + 1) * rows)
        values.append(dot(acc[own], vue_ref[h]))
        for k, row in enumerate(pieces(top[:, own], 3) + pieces(total[:, own], 2)):
            tail = jnp.where(line == 8 * h + k, row, tail)
    return jnp.concatenate(values + [tail.T], axis=1)


def merge(parts, tails):
    nums, tops, totals = [], [], []
    for h in range(H_DEV):
        stats = [stats_of(t, h) for t in tails]
        top = stats[0][0]
        for m, _ in stats[1:]:
            top = jnp.maximum(top, m)
        num, total = 0.0, 0.0
        for part, (m, l) in zip(parts, stats):
            f = jnp.exp2((m - top) * COEF)
            num = num + part[:, h * VD : (h + 1) * VD] * f
            total = total + l * f
        nums.append(num)
        tops.append(top)
        totals.append(total)
    return nums, tops, totals


def merge_half(in_ref, out_ref):
    n, rows, _ = in_ref.shape
    data = [in_ref[s].astype(F32) for s in range(n)]
    nums, tops, totals = merge([d[:, : H_DEV * VD] for d in data], [d[:, H_DEV * VD :] for d in data])
    out_ref[...] = jnp.concatenate(nums + [with_stats(tops, totals, rows)], axis=1).astype(BF)


def merge_all(own_ref, other_ref, shard_ref, out_ref):
    n = own_ref.shape[0] // 2
    other = other_ref[...].astype(F32)
    data = [own_ref[...].astype(F32), jnp.concatenate([other[n:], other[:n]], axis=0)]
    nums, _, totals = merge([d[:, : H_DEV * VD] for d in data], [d[:, H_DEV * VD :] for d in data])
    value = jnp.concatenate([a / t for a, t in zip(nums, totals)], axis=1)
    swapped = jnp.concatenate([value[n:], value[:n]], axis=0)
    value = jnp.where(shard_ref[1] == 0, value, swapped).astype(BF)
    for k in range(out_ref.shape[0]):
        out_ref[k] = value


def project(value_ref, w_ref, out_ref):
    res = nt_dot(value_ref[...], w_ref[...])
    order = [res[(c * 8 + xz) * 8 : (c * 8 + xz) * 8 + 8] for xz in range(8) for c in range(2)]
    out_ref[...] = jnp.concatenate(order, axis=0).astype(BF)


def call(kernel, out_shape, *args, scratch=(), spaces=None, limit=16):
    return pl.pallas_call(
        kernel,
        out_shape=out_shape,
        in_specs=[pl.BlockSpec(memory_space=m) for m in spaces or [pltpu.VMEM] * len(args)],
        out_specs=pl.BlockSpec(memory_space=pltpu.VMEM),
        scratch_shapes=list(scratch),
        compiler_params=pltpu.CompilerParams(vmem_limit_bytes=limit * 2**20),
        interpret=INTERPRET,
    )(*args)


def body(queries, w_uk, value_up_weight, w_out, kv_cache, blocks):
    n_ctx = lax.axis_size("ctx")
    n_half = n_ctx // 2
    shard = lax.axis_index("ctx")
    place = jnp.stack([shard, (shard // 2) % 2]).astype(jnp.int32)
    near_q = jnp.broadcast_to(queries[None], (n_half,) + queries.shape)
    near_q = lax.all_to_all(near_q, "ctx", 0, 0, axis_index_groups=SAME_HALF)
    near_q = near_q.reshape(ROWS // 2, -1)
    keys, near_bias, far_bias = staged(kv_cache, blocks.T, place)
    near_q, near_bias = lax.optimization_barrier((near_q, near_bias))
    far_q = lax.ppermute(near_q, "ctx", OTHER_HALF)
    keys = in_hbm(keys)
    width = H_DEV * ROWS // 2
    scratch = [
        pltpu.VMEM((WIDE, width), BF),
        pltpu.VMEM((keys.shape[0], width), F32),
        pltpu.VMEM((keys.shape[0], width), BF),
        pltpu.VMEM(keys.shape, BF),
        pltpu.SemaphoreType.DMA((len(PARTS),)),
    ]
    own = ROWS // n_half
    near = call(
        attend_near,
        jax.ShapeDtypeStruct((ROWS // 2, WIDE), BF),
        near_q, w_uk, value_up_weight, near_bias, keys,
        scratch=scratch,
        spaces=[pltpu.VMEM] * 4 + [pltpu.HBM],
        limit=40,
    )
    parts = call(
        attend_far,
        jax.ShapeDtypeStruct((n_half, own, WIDE), BF),
        far_q, w_uk, value_up_weight, far_bias, near, keys,
        scratch=scratch,
        spaces=[pltpu.VMEM] * 5 + [pltpu.HBM],
        limit=40,
    )
    parts = lax.all_to_all(parts, "ctx", 0, 0, axis_index_groups=SAME_HALF)
    half = call(merge_half, jax.ShapeDtypeStruct((own, WIDE), BF), parts)
    other = lax.ppermute(half, "ctx", OTHER_HALF)
    value = call(
        merge_all,
        jax.ShapeDtypeStruct((n_half, own, H_DEV * VD), BF),
        half, other, place,
        spaces=[pltpu.VMEM] * 2 + [pltpu.SMEM],
    )
    value = lax.all_to_all(value, "ctx", 0, 0, axis_index_groups=SAME_HALF).reshape(ROWS, -1)
    partial = call(project, jax.ShapeDtypeStruct((ROWS, w_out.shape[1]), BF), value, w_out.T)
    n_head = lax.axis_size("head")
    shares = lax.all_to_all(partial.reshape(n_head, ROWS // n_head, -1), "head", 0, 0)
    return jnp.sum(shares.astype(F32), axis=0).astype(BF)


def solution(mesh):
    return jax.shard_map(
        body,
        mesh=mesh,
        in_specs=(
            P("ctx", "head"),
            P("head", None, None),
            P("head", None, None),
            P("head", "ctx"),
            P("ctx", None),
            P(),
        ),
        out_specs=P("head", "ctx"),
        check_vma=False,
    )
```

```python
import numpy as np
import jax
import jax.numpy as jnp
from jax import lax
from jax.experimental import pallas as pl
from jax.experimental.pallas import tpu as pltpu
from jax.sharding import PartitionSpec as P

BF = jnp.bfloat16
F32 = jnp.float32
NEG = -1e30
H_DEV = 4
ROWS = 128
NOPE = 128
ROPE = 64
KVR = 512
VD = 128
BLOCK = 64
WIDE = 640
PAIR = 1152
PARTS = (0.125, 0.25, 0.3125, 0.3125)
CHUNK = 256
STAGE_PAIRS = 4
COEF = float((NOPE + ROPE) ** -0.5 * np.log2(np.e))
INTERPRET = False
KEY = KVR + ROPE

SAME_HALF = [[x * 4 + z * 2 + c for c in range(2) for x in range(4)] for z in range(2)]
OTHER_HALF = [(i, i ^ 2) for i in range(16)]


def nt_dot(a, b):
    return lax.dot_general(a, b, (((1,), (1,)), ((), ())), preferred_element_type=F32)


def dot(a, b):
    return jnp.dot(a, b, preferred_element_type=F32)


def tn_dot(a, b):
    return lax.dot_general(a, b, (((0,), (0,)), ((), ())), preferred_element_type=F32)


def pieces(x, n):
    out = []
    for _ in range(n):
        part = x.astype(BF).astype(F32)
        out.append(part)
        x = x - part
    return out


def with_stats(tops, totals, rows):
    lane = lax.broadcasted_iota(jnp.int32, (rows, 128), 1)
    tail = jnp.zeros((rows, 128), F32)
    for h in range(H_DEV):
        cols = pieces(tops[h], 3) + pieces(totals[h], 2)
        for k, col in enumerate(cols):
            tail = jnp.where(lane == 8 * h + k, col, tail)
    return tail


def stats_of(tail, h):
    t = tail[:, 8 * h : 8 * h + 8]
    top = t[:, 0:1] + (t[:, 1:2] + t[:, 2:3])
    return top, t[:, 3:4] + t[:, 4:5]


def in_hbm(x):
    return pltpu.with_memory_space_constraint(x, pltpu.HBM)


def stage(kv_hbm, blocks_hbm, shard_ref, out_hbm, bias_ref, kv_ref, blocks_ref, keys_ref, sems, sent):
    count, lanes = kv_ref.shape
    span = STAGE_PAIRS * PAIR
    chunk = STAGE_PAIRS * 2 * count
    steps = lanes // span
    got = []
    for i in range(steps):
        at = pl.ds(i * span, span)
        got.append(pltpu.make_async_copy(kv_hbm.at[:, at], kv_ref.at[:, at], sems.at[i]))
        got[-1].start()
    table = pltpu.make_async_copy(blocks_hbm, blocks_ref, sems.at[steps])
    table.start()
    pad = jnp.zeros((count, WIDE - KEY), BF)
    put = []
    for i in range(steps):
        got[i].wait()
        for t in range(STAGE_PAIRS):
            pair = kv_ref[:, i * span + t * PAIR : i * span + (t + 1) * PAIR]
            for o in range(2):
                key = jnp.concatenate([pair[:, o * KEY : (o + 1) * KEY], pad], axis=1)
                first = i * chunk + (2 * t + o) * count
                keys_ref[first : first + count, :] = key
        at = pl.ds(i * chunk, chunk)
        put.append(pltpu.make_async_copy(keys_ref.at[at], out_hbm.at[at], sent.at[i]))
        put[-1].start()
    table.wait()
    b = blocks_ref[...]
    n = ROWS // 16
    order = [xz * 2 + c for c in range(2) for xz in range(8)]
    b = jnp.concatenate([b[:, k * n : (k + 1) * n] for k in order], axis=1)
    b = b - shard_ref[0] * count
    line = lax.broadcasted_iota(jnp.int32, (count, ROWS), 0)
    bias = jnp.full((count, ROWS), NEG, F32)
    for k in range(b.shape[0]):
        bias = jnp.where(b[k : k + 1, :] == line, 0.0, bias)
    bias_ref[...] = jnp.concatenate([bias, bias], axis=0)
    for copy in put:
        copy.wait()


def staged(kv, blocks, shard):
    steps = kv.shape[1] // (PAIR * STAGE_PAIRS)
    keys = (kv.shape[0] * kv.shape[1] // KEY, WIDE)
    return pl.pallas_call(
        stage,
        out_shape=(pltpu.HBM(keys, BF), jax.ShapeDtypeStruct((2 * kv.shape[0], ROWS), F32)),
        in_specs=[
            pl.BlockSpec(memory_space=pltpu.HBM),
            pl.BlockSpec(memory_space=pltpu.HBM),
            pl.BlockSpec(memory_space=pltpu.SMEM),
        ],
        out_specs=(pl.BlockSpec(memory_space=pltpu.HBM), pl.BlockSpec(memory_space=pltpu.VMEM)),
        scratch_shapes=[
            pltpu.VMEM(kv.shape, BF),
            pltpu.VMEM(blocks.shape, jnp.int32),
            pltpu.VMEM(keys, BF),
            pltpu.SemaphoreType.DMA((steps + 1,)),
            pltpu.SemaphoreType.DMA((steps,)),
        ],
        compiler_params=pltpu.CompilerParams(vmem_limit_bytes=24 * 2**20),
        interpret=INTERPRET,
    )(in_hbm(kv), in_hbm(blocks), shard)


def attend(q_ref, w_ref, vue_ref, bias_ref, k_hbm, out_ref, qt, s_ref, p_ref, k_ref, sems):
    width = qt.shape[1]
    rows = width // H_DEV
    bounds = [0]
    for share in PARTS:
        bounds.append(bounds[-1] + int(share * k_ref.shape[0]))
    spans = list(zip(bounds, bounds[1:]))
    copies = []
    for n, (a, b) in enumerate(spans):
        span = pl.ds(a, b - a)
        copies.append(pltpu.make_async_copy(k_hbm.at[span], k_ref.at[span], sems.at[n]))
        copies[-1].start()
    qt[KEY:, :] = jnp.zeros((WIDE - KEY, width), BF)
    for h in range(H_DEV):
        own = slice(h * rows, (h + 1) * rows)
        q = q_ref[:, h * (NOPE + ROPE) : (h + 1) * (NOPE + ROPE)]
        absorbed = lax.dot_general(
            w_ref[h], q[:, :NOPE], (((0,), (1,)), ((), ())), preferred_element_type=F32
        )
        qt[:KVR, own] = absorbed.astype(BF)
        qt[KVR:KEY, own] = q[:, NOPE:].T

    def score(first, top):
        s = dot(k_ref[first : first + CHUNK, :], qt[...])
        for at in range(0, CHUNK, 128):
            piece = s[at : at + 128, :] + jnp.concatenate([bias_ref[...]] * H_DEV, axis=1)
            top = jnp.maximum(top, jnp.max(piece.reshape(16, 8, width), axis=0))
            s_ref[first + at : first + at + 128, :] = piece
        return top

    def weigh(first, top, total):
        for at in range(first, first + CHUNK, 128):
            w = jnp.exp2((s_ref[at : at + 128, :] - top) * COEF)
            total = total + jnp.sum(w.reshape(16, 8, width), axis=0)
            p_ref[at : at + 128, :] = w.astype(BF)
        return total

    lowest = jnp.full((8, width), NEG, F32)
    tops, totals, accs = [], [], []
    copies[0].wait()
    top = lowest
    for first in range(spans[0][0], spans[0][1], CHUNK):
        top = score(first, top)
    tops.append(jnp.max(top, axis=0, keepdims=True))
    for n, (a, b) in enumerate(spans):
        total = jnp.zeros((8, width), F32)
        top = lowest
        now = list(range(a, b, CHUNK))
        later = []
        if n + 1 < len(spans):
            copies[n + 1].wait()
            later = list(range(spans[n + 1][0], spans[n + 1][1], CHUNK))
        while now or later:
            if later:
                top = score(later.pop(0), top)
            if now:
                total = weigh(now.pop(0), tops[n], total)
        if n + 1 < len(spans):
            tops.append(jnp.max(top, axis=0, keepdims=True))
        totals.append(jnp.sum(total, axis=0, keepdims=True))
        accs.append(tn_dot(p_ref[a:b, :], k_ref[a:b, :KVR]))
    top = tops[0]
    for t in tops[1:]:
        top = jnp.maximum(top, t)
    acc, total = 0.0, 0.0
    for a, t, l in zip(accs, tops, totals):
        f = jnp.exp2((t - top) * COEF)
        acc = acc + a * f.reshape(width, 1)
        total = total + f * l
    acc = acc.astype(BF)
    line = lax.broadcasted_iota(jnp.int32, (128, rows), 0)
    tail = jnp.zeros((128, rows), F32)
    for h in range(H_DEV):
        own = slice(h * rows, (h + 1) * rows)
        out_ref[:, h * VD : (h + 1) * VD] = dot(acc[own], vue_ref[h]).astype(BF)
        for k, row in enumerate(pieces(top[:, own], 3) + pieces(total[:, own], 2)):
            tail = jnp.where(line == 8 * h + k, row, tail)
    out_ref[:, H_DEV * VD :] = tail.T.astype(BF)


def merge(parts, tails):
    nums, tops, totals = [], [], []
    for h in range(H_DEV):
        stats = [stats_of(t, h) for t in tails]
        top = stats[0][0]
        for m, _ in stats[1:]:
            top = jnp.maximum(top, m)
        num, total = 0.0, 0.0
        for part, (m, l) in zip(parts, stats):
            f = jnp.exp2((m - top) * COEF)
            num = num + part[:, h * VD : (h + 1) * VD] * f
            total = total + l * f
        nums.append(num)
        tops.append(top)
        totals.append(total)
    return nums, tops, totals


def merge_half(in_ref, out_ref):
    n, rows, _ = in_ref.shape
    data = [in_ref[s].astype(F32) for s in range(n)]
    nums, tops, totals = merge([d[:, : H_DEV * VD] for d in data], [d[:, H_DEV * VD :] for d in data])
    out_ref[...] = jnp.concatenate(nums + [with_stats(tops, totals, rows)], axis=1).astype(BF)


def copies_of_both(own_ref, other_ref, place_ref, out_ref):
    own, other = own_ref[...].astype(F32), other_ref[...].astype(F32)
    lower = place_ref[1] == 0
    first, second = jnp.where(lower, own, other), jnp.where(lower, other, own)
    both = jnp.concatenate([first, second], axis=0).astype(BF)
    for k in range(out_ref.shape[0]):
        out_ref[k] = both


def merge_all(own_ref, other_ref, out_ref):
    data = [own_ref[...].astype(F32), other_ref[...].astype(F32)]
    nums, _, totals = merge([d[:, : H_DEV * VD] for d in data], [d[:, H_DEV * VD :] for d in data])
    value = jnp.concatenate([n / t for n, t in zip(nums, totals)], axis=1).astype(BF)
    for k in range(out_ref.shape[0]):
        out_ref[k] = value


def project(value_ref, w_ref, out_ref):
    res = nt_dot(value_ref[...], w_ref[...])
    order = [res[(c * 8 + xz) * 8 : (c * 8 + xz) * 8 + 8] for xz in range(8) for c in range(2)]
    out_ref[...] = jnp.concatenate(order, axis=0).astype(BF)


def call(kernel, out_shape, *args, scratch=(), spaces=None, limit=16):
    return pl.pallas_call(
        kernel,
        out_shape=out_shape,
        in_specs=[pl.BlockSpec(memory_space=m) for m in spaces or [pltpu.VMEM] * len(args)],
        out_specs=pl.BlockSpec(memory_space=pltpu.VMEM),
        scratch_shapes=list(scratch),
        compiler_params=pltpu.CompilerParams(vmem_limit_bytes=limit * 2**20),
        interpret=INTERPRET,
    )(*args)


def body(queries, w_uk, value_up_weight, w_out, kv_cache, blocks):
    n_ctx = lax.axis_size("ctx")
    n_half = n_ctx // 2
    own = 2 * queries.shape[0]
    shard = lax.axis_index("ctx")
    place = jnp.stack([shard, (shard // 2) % 2]).astype(jnp.int32)
    other = lax.ppermute(queries, "ctx", OTHER_HALF)
    keys, bias = staged(kv_cache, blocks.T, place)
    both = call(
        copies_of_both,
        jax.ShapeDtypeStruct((n_half, own, queries.shape[1]), BF),
        queries, other, place,
        spaces=[pltpu.VMEM] * 2 + [pltpu.SMEM],
    )
    q = lax.all_to_all(both, "ctx", 0, 0, axis_index_groups=SAME_HALF).reshape(ROWS, -1)
    width = H_DEV * ROWS
    parts = call(
        attend,
        jax.ShapeDtypeStruct((ROWS, WIDE), BF),
        q, w_uk, value_up_weight, bias, in_hbm(keys),
        scratch=[
            pltpu.VMEM((WIDE, width), BF),
            pltpu.VMEM((keys.shape[0], width), F32),
            pltpu.VMEM((keys.shape[0], width), BF),
            pltpu.VMEM(keys.shape, BF),
            pltpu.SemaphoreType.DMA((len(PARTS),)),
        ],
        spaces=[pltpu.VMEM] * 4 + [pltpu.HBM],
        limit=40,
    )
    parts = lax.all_to_all(
        parts.reshape(n_half, own, WIDE), "ctx", 0, 0, axis_index_groups=SAME_HALF
    )
    half = call(merge_half, jax.ShapeDtypeStruct((own, WIDE), BF), parts)
    other = lax.ppermute(half, "ctx", OTHER_HALF)
    value = call(merge_all, jax.ShapeDtypeStruct((n_half, own, H_DEV * VD), BF), half, other)
    value = lax.all_to_all(value, "ctx", 0, 0, axis_index_groups=SAME_HALF).reshape(ROWS, -1)
    partial = call(project, jax.ShapeDtypeStruct((ROWS, w_out.shape[1]), BF), value, w_out.T)
    n_head = lax.axis_size("head")
    shares = lax.all_to_all(partial.reshape(n_head, ROWS // n_head, -1), "head", 0, 0)
    return jnp.sum(shares.astype(F32), axis=0).astype(BF)


def solution(mesh):
    return jax.shard_map(
        body,
        mesh=mesh,
        in_specs=(
            P("ctx", "head"),
            P("head", None, None),
            P("head", None, None),
            P("head", "ctx"),
            P("ctx", None),
            P(),
        ),
        out_specs=P("head", "ctx"),
        check_vma=False,
    )
```

```python
import numpy as np
import jax
import jax.numpy as jnp
from jax import lax
from jax.experimental import pallas as pl
from jax.experimental.pallas import tpu as pltpu
from jax.sharding import PartitionSpec as P

BF = jnp.bfloat16
F32 = jnp.float32
NEG = -1e30
H_DEV = 4
ROWS = 128
NOPE = 128
ROPE = 64
KVR = 512
VD = 128
BLOCK = 64
WIDE = 640
PAIR = 1152
PARTS = (0.125, 0.25, 0.3125, 0.3125)
CHUNK = 256
STAGE_PAIRS = 4
COEF = float((NOPE + ROPE) ** -0.5 * np.log2(np.e))
INTERPRET = False
KEY = KVR + ROPE

SAME_HALF = [[x * 4 + z * 2 + c for c in range(2) for x in range(4)] for z in range(2)]
OTHER_HALF = [(i, i ^ 2) for i in range(16)]


def nt_dot(a, b):
    return lax.dot_general(a, b, (((1,), (1,)), ((), ())), preferred_element_type=F32)


def dot(a, b):
    return jnp.dot(a, b, preferred_element_type=F32)


def tn_dot(a, b):
    return lax.dot_general(a, b, (((0,), (0,)), ((), ())), preferred_element_type=F32)


def pieces(x, n):
    out = []
    for _ in range(n):
        part = x.astype(BF).astype(F32)
        out.append(part)
        x = x - part
    return out


def with_stats(tops, totals, rows):
    lane = lax.broadcasted_iota(jnp.int32, (rows, 128), 1)
    tail = jnp.zeros((rows, 128), F32)
    for h in range(H_DEV):
        cols = pieces(tops[h], 3) + pieces(totals[h], 2)
        for k, col in enumerate(cols):
            tail = jnp.where(lane == 8 * h + k, col, tail)
    return tail


def stats_of(tail, h):
    t = tail[:, 8 * h : 8 * h + 8]
    top = t[:, 0:1] + (t[:, 1:2] + t[:, 2:3])
    return top, t[:, 3:4] + t[:, 4:5]


def in_hbm(x):
    return pltpu.with_memory_space_constraint(x, pltpu.HBM)


def stage(
    kv_hbm, blocks_hbm, q_hbm, shard_ref, out_hbm, bias_ref, q_ref, kv_ref, blocks_ref, keys_ref, sems, sent
):
    count, lanes = kv_ref.shape
    span = STAGE_PAIRS * PAIR
    chunk = STAGE_PAIRS * 2 * count
    steps = lanes // span
    got = []
    for i in range(steps):
        at = pl.ds(i * span, span)
        got.append(pltpu.make_async_copy(kv_hbm.at[:, at], kv_ref.at[:, at], sems.at[i]))
        got[-1].start()
    table = pltpu.make_async_copy(blocks_hbm, blocks_ref, sems.at[steps])
    table.start()
    own = pltpu.make_async_copy(q_hbm, q_ref, sems.at[steps + 1])
    own.start()
    pad = jnp.zeros((count, WIDE - KEY), BF)
    put = []
    for i in range(steps):
        got[i].wait()
        for t in range(STAGE_PAIRS):
            pair = kv_ref[:, i * span + t * PAIR : i * span + (t + 1) * PAIR]
            for o in range(2):
                key = jnp.concatenate([pair[:, o * KEY : (o + 1) * KEY], pad], axis=1)
                first = i * chunk + (2 * t + o) * count
                keys_ref[first : first + count, :] = key
        at = pl.ds(i * chunk, chunk)
        put.append(pltpu.make_async_copy(keys_ref.at[at], out_hbm.at[at], sent.at[i]))
        put[-1].start()
    table.wait()
    b = blocks_ref[...]
    n = ROWS // 16
    order = [xz * 2 + c for c in range(2) for xz in range(8)]
    b = jnp.concatenate([b[:, k * n : (k + 1) * n] for k in order], axis=1)
    b = b - shard_ref[0] * count
    line = lax.broadcasted_iota(jnp.int32, (count, ROWS), 0)
    bias = jnp.full((count, ROWS), NEG, F32)
    for k in range(b.shape[0]):
        bias = jnp.where(b[k : k + 1, :] == line, 0.0, bias)
    bias_ref[...] = jnp.concatenate([bias, bias], axis=0)
    own.wait()
    for copy in put:
        copy.wait()


def staged(kv, blocks, queries, shard):
    steps = kv.shape[1] // (PAIR * STAGE_PAIRS)
    keys = (kv.shape[0] * kv.shape[1] // KEY, WIDE)
    return pl.pallas_call(
        stage,
        out_shape=(
            pltpu.HBM(keys, BF),
            jax.ShapeDtypeStruct((2 * kv.shape[0], ROWS), F32),
            jax.ShapeDtypeStruct(queries.shape, BF),
        ),
        in_specs=[
            pl.BlockSpec(memory_space=pltpu.HBM),
            pl.BlockSpec(memory_space=pltpu.HBM),
            pl.BlockSpec(memory_space=pltpu.HBM),
            pl.BlockSpec(memory_space=pltpu.SMEM),
        ],
        out_specs=(
            pl.BlockSpec(memory_space=pltpu.HBM),
            pl.BlockSpec(memory_space=pltpu.VMEM),
            pl.BlockSpec(memory_space=pltpu.VMEM),
        ),
        scratch_shapes=[
            pltpu.VMEM(kv.shape, BF),
            pltpu.VMEM(blocks.shape, jnp.int32),
            pltpu.VMEM(keys, BF),
            pltpu.SemaphoreType.DMA((steps + 2,)),
            pltpu.SemaphoreType.DMA((steps,)),
        ],
        compiler_params=pltpu.CompilerParams(vmem_limit_bytes=24 * 2**20),
        interpret=INTERPRET,
    )(in_hbm(kv), in_hbm(blocks), in_hbm(queries), shard)


def attend(q_ref, w_ref, vue_ref, bias_ref, k_hbm, out_ref, qt, s_ref, p_ref, k_ref, sems):
    width = qt.shape[1]
    rows = width // H_DEV
    bounds = [0]
    for share in PARTS:
        bounds.append(bounds[-1] + int(share * k_ref.shape[0]))
    spans = list(zip(bounds, bounds[1:]))
    copies = []
    for n, (a, b) in enumerate(spans):
        span = pl.ds(a, b - a)
        copies.append(pltpu.make_async_copy(k_hbm.at[span], k_ref.at[span], sems.at[n]))
        copies[-1].start()
    qt[KEY:, :] = jnp.zeros((WIDE - KEY, width), BF)
    for h in range(H_DEV):
        own = slice(h * rows, (h + 1) * rows)
        q = q_ref[:, h * (NOPE + ROPE) : (h + 1) * (NOPE + ROPE)]
        absorbed = lax.dot_general(
            w_ref[h], q[:, :NOPE], (((0,), (1,)), ((), ())), preferred_element_type=F32
        )
        qt[:KVR, own] = absorbed.astype(BF)
        qt[KVR:KEY, own] = q[:, NOPE:].T

    def score(first, top):
        s = dot(k_ref[first : first + CHUNK, :], qt[...])
        for at in range(0, CHUNK, 128):
            piece = s[at : at + 128, :] + jnp.concatenate([bias_ref[...]] * H_DEV, axis=1)
            top = jnp.maximum(top, jnp.max(piece.reshape(16, 8, width), axis=0))
            s_ref[first + at : first + at + 128, :] = piece
        return top

    def weigh(first, top, total):
        for at in range(first, first + CHUNK, 128):
            w = jnp.exp2((s_ref[at : at + 128, :] - top) * COEF)
            total = total + jnp.sum(w.reshape(16, 8, width), axis=0)
            p_ref[at : at + 128, :] = w.astype(BF)
        return total

    lowest = jnp.full((8, width), NEG, F32)
    tops, totals, accs = [], [], []
    copies[0].wait()
    top = lowest
    for first in range(spans[0][0], spans[0][1], CHUNK):
        top = score(first, top)
    tops.append(jnp.max(top, axis=0, keepdims=True))
    for n, (a, b) in enumerate(spans):
        total = jnp.zeros((8, width), F32)
        top = lowest
        now = list(range(a, b, CHUNK))
        later = []
        if n + 1 < len(spans):
            copies[n + 1].wait()
            later = list(range(spans[n + 1][0], spans[n + 1][1], CHUNK))
        while now or later:
            if later:
                top = score(later.pop(0), top)
            if now:
                total = weigh(now.pop(0), tops[n], total)
        if n + 1 < len(spans):
            tops.append(jnp.max(top, axis=0, keepdims=True))
        totals.append(jnp.sum(total, axis=0, keepdims=True))
        accs.append(tn_dot(p_ref[a:b, :], k_ref[a:b, :KVR]))
    top = tops[0]
    for t in tops[1:]:
        top = jnp.maximum(top, t)
    acc, total = 0.0, 0.0
    for a, t, l in zip(accs, tops, totals):
        f = jnp.exp2((t - top) * COEF)
        acc = acc + a * f.reshape(width, 1)
        total = total + f * l
    acc = acc.astype(BF)
    line = lax.broadcasted_iota(jnp.int32, (128, rows), 0)
    tail = jnp.zeros((128, rows), F32)
    for h in range(H_DEV):
        own = slice(h * rows, (h + 1) * rows)
        out_ref[:, h * VD : (h + 1) * VD] = dot(acc[own], vue_ref[h]).astype(BF)
        for k, row in enumerate(pieces(top[:, own], 3) + pieces(total[:, own], 2)):
            tail = jnp.where(line == 8 * h + k, row, tail)
    out_ref[:, H_DEV * VD :] = tail.T.astype(BF)


def merge(parts, tails):
    nums, tops, totals = [], [], []
    for h in range(H_DEV):
        stats = [stats_of(t, h) for t in tails]
        top = stats[0][0]
        for m, _ in stats[1:]:
            top = jnp.maximum(top, m)
        num, total = 0.0, 0.0
        for part, (m, l) in zip(parts, stats):
            f = jnp.exp2((m - top) * COEF)
            num = num + part[:, h * VD : (h + 1) * VD] * f
            total = total + l * f
        nums.append(num)
        tops.append(top)
        totals.append(total)
    return nums, tops, totals


def merge_half(in_ref, out_ref):
    n, rows, _ = in_ref.shape
    data = [in_ref[s].astype(F32) for s in range(n)]
    nums, tops, totals = merge([d[:, : H_DEV * VD] for d in data], [d[:, H_DEV * VD :] for d in data])
    out_ref[...] = jnp.concatenate(nums + [with_stats(tops, totals, rows)], axis=1).astype(BF)


def copies_of_both(own_ref, other_ref, place_ref, out_ref):
    own, other = own_ref[...].astype(F32), other_ref[...].astype(F32)
    lower = place_ref[1] == 0
    first, second = jnp.where(lower, own, other), jnp.where(lower, other, own)
    both = jnp.concatenate([first, second], axis=0).astype(BF)
    for k in range(out_ref.shape[0]):
        out_ref[k] = both


def merge_all(own_ref, other_ref, out_ref):
    data = [own_ref[...].astype(F32), other_ref[...].astype(F32)]
    nums, _, totals = merge([d[:, : H_DEV * VD] for d in data], [d[:, H_DEV * VD :] for d in data])
    value = jnp.concatenate([n / t for n, t in zip(nums, totals)], axis=1).astype(BF)
    for k in range(out_ref.shape[0]):
        out_ref[k] = value


def project(value_ref, w_ref, out_ref):
    res = nt_dot(value_ref[...], w_ref[...])
    order = [res[(c * 8 + xz) * 8 : (c * 8 + xz) * 8 + 8] for xz in range(8) for c in range(2)]
    out_ref[...] = jnp.concatenate(order, axis=0).astype(BF)


def call(kernel, out_shape, *args, scratch=(), spaces=None, limit=16):
    return pl.pallas_call(
        kernel,
        out_shape=out_shape,
        in_specs=[pl.BlockSpec(memory_space=m) for m in spaces or [pltpu.VMEM] * len(args)],
        out_specs=pl.BlockSpec(memory_space=pltpu.VMEM),
        scratch_shapes=list(scratch),
        compiler_params=pltpu.CompilerParams(vmem_limit_bytes=limit * 2**20),
        interpret=INTERPRET,
    )(*args)


def body(queries, w_uk, value_up_weight, w_out, kv_cache, blocks):
    n_ctx = lax.axis_size("ctx")
    n_half = n_ctx // 2
    own = 2 * queries.shape[0]
    shard = lax.axis_index("ctx")
    place = jnp.stack([shard, (shard // 2) % 2]).astype(jnp.int32)
    other = lax.ppermute(queries, "ctx", OTHER_HALF)
    keys, bias, queries = staged(kv_cache, blocks.T, queries, place)
    other, bias = lax.optimization_barrier((other, bias))
    both = call(
        copies_of_both,
        jax.ShapeDtypeStruct((n_half, own, queries.shape[1]), BF),
        queries, other, place,
        spaces=[pltpu.VMEM] * 2 + [pltpu.SMEM],
    )
    q = lax.all_to_all(both, "ctx", 0, 0, axis_index_groups=SAME_HALF).reshape(ROWS, -1)
    width = H_DEV * ROWS
    parts = call(
        attend,
        jax.ShapeDtypeStruct((ROWS, WIDE), BF),
        q, w_uk, value_up_weight, bias, in_hbm(keys),
        scratch=[
            pltpu.VMEM((WIDE, width), BF),
            pltpu.VMEM((keys.shape[0], width), F32),
            pltpu.VMEM((keys.shape[0], width), BF),
            pltpu.VMEM(keys.shape, BF),
            pltpu.SemaphoreType.DMA((len(PARTS),)),
        ],
        spaces=[pltpu.VMEM] * 4 + [pltpu.HBM],
        limit=40,
    )
    parts = lax.all_to_all(
        parts.reshape(n_half, own, WIDE), "ctx", 0, 0, axis_index_groups=SAME_HALF
    )
    half = call(merge_half, jax.ShapeDtypeStruct((own, WIDE), BF), parts)
    other = lax.ppermute(half, "ctx", OTHER_HALF)
    value = call(merge_all, jax.ShapeDtypeStruct((n_half, own, H_DEV * VD), BF), half, other)
    value = lax.all_to_all(value, "ctx", 0, 0, axis_index_groups=SAME_HALF).reshape(ROWS, -1)
    partial = call(project, jax.ShapeDtypeStruct((ROWS, w_out.shape[1]), BF), value, w_out.T)
    n_head = lax.axis_size("head")
    shares = lax.all_to_all(partial.reshape(n_head, ROWS // n_head, -1), "head", 0, 0)
    return jnp.sum(shares.astype(F32), axis=0).astype(BF)


def solution(mesh):
    return jax.shard_map(
        body,
        mesh=mesh,
        in_specs=(
            P("ctx", "head"),
            P("head", None, None),
            P("head", None, None),
            P("head", "ctx"),
            P("ctx", None),
            P(),
        ),
        out_specs=P("head", "ctx"),
        check_vma=False,
    )
```

```python
import numpy as np
import jax
import jax.numpy as jnp
from jax import lax
from jax.experimental import pallas as pl
from jax.experimental.pallas import tpu as pltpu
from jax.sharding import PartitionSpec as P

BF = jnp.bfloat16
F32 = jnp.float32
NEG = -1e30
H_DEV = 4
ROWS = 128
NOPE = 128
ROPE = 64
KVR = 512
VD = 128
BLOCK = 64
WIDE = 640
PAIR = 1152
PARTS = (0.25, 0.25, 0.25, 0.25)
CHUNK = 256
STAGE_PAIRS = 4
COEF = float((NOPE + ROPE) ** -0.5 * np.log2(np.e))
INTERPRET = False
KEY = KVR + ROPE

SAME_HALF = [[x * 4 + z * 2 + c for c in range(2) for x in range(4)] for z in range(2)]
OTHER_HALF = [(i, i ^ 2) for i in range(16)]


def nt_dot(a, b):
    return lax.dot_general(a, b, (((1,), (1,)), ((), ())), preferred_element_type=F32)


def dot(a, b):
    return jnp.dot(a, b, preferred_element_type=F32)


def tn_dot(a, b):
    return lax.dot_general(a, b, (((0,), (0,)), ((), ())), preferred_element_type=F32)


def pieces(x, n):
    out = []
    for _ in range(n):
        part = x.astype(BF).astype(F32)
        out.append(part)
        x = x - part
    return out


def with_stats(tops, totals, rows):
    lane = lax.broadcasted_iota(jnp.int32, (rows, 128), 1)
    tail = jnp.zeros((rows, 128), F32)
    for h in range(H_DEV):
        cols = pieces(tops[h], 3) + pieces(totals[h], 2)
        for k, col in enumerate(cols):
            tail = jnp.where(lane == 8 * h + k, col, tail)
    return tail


def stats_of(tail, h):
    t = tail[:, 8 * h : 8 * h + 8]
    top = t[:, 0:1] + (t[:, 1:2] + t[:, 2:3])
    return top, t[:, 3:4] + t[:, 4:5]


def in_hbm(x):
    return pltpu.with_memory_space_constraint(x, pltpu.HBM)


def stage(
    kv_hbm, blocks_hbm, q_hbm, shard_ref, out_hbm, bias_ref, q_ref, head_ref, kv_ref, blocks_ref, keys_ref,
    sems, sent,
):
    count, lanes = kv_ref.shape
    span = STAGE_PAIRS * PAIR
    chunk = STAGE_PAIRS * 2 * count
    steps = lanes // span
    got = []
    for i in range(steps):
        at = pl.ds(i * span, span)
        got.append(pltpu.make_async_copy(kv_hbm.at[:, at], kv_ref.at[:, at], sems.at[i]))
        got[-1].start()
    table = pltpu.make_async_copy(blocks_hbm, blocks_ref, sems.at[steps])
    table.start()
    own = pltpu.make_async_copy(q_hbm, q_ref, sems.at[steps + 1])
    own.start()
    pad = jnp.zeros((count, WIDE - KEY), BF)
    put = []
    for i in range(steps):
        got[i].wait()
        for t in range(STAGE_PAIRS):
            pair = kv_ref[:, i * span + t * PAIR : i * span + (t + 1) * PAIR]
            for o in range(2):
                key = jnp.concatenate([pair[:, o * KEY : (o + 1) * KEY], pad], axis=1)
                first = i * chunk + (2 * t + o) * count
                keys_ref[first : first + count, :] = key
                if first < head_ref.shape[0]:
                    head_ref[first : first + count, :] = key
        at = pl.ds(i * chunk, chunk)
        put.append(pltpu.make_async_copy(keys_ref.at[at], out_hbm.at[at], sent.at[i]))
        put[-1].start()
    table.wait()
    b = blocks_ref[...]
    n = ROWS // 16
    order = [xz * 2 + c for c in range(2) for xz in range(8)]
    b = jnp.concatenate([b[:, k * n : (k + 1) * n] for k in order], axis=1)
    b = b - shard_ref[0] * count
    line = lax.broadcasted_iota(jnp.int32, (count, ROWS), 0)
    bias = jnp.full((count, ROWS), NEG, F32)
    for k in range(b.shape[0]):
        bias = jnp.where(b[k : k + 1, :] == line, 0.0, bias)
    bias_ref[...] = jnp.concatenate([bias, bias], axis=0)
    own.wait()
    for copy in put:
        copy.wait()


def staged(kv, blocks, queries, shard):
    steps = kv.shape[1] // (PAIR * STAGE_PAIRS)
    keys = (kv.shape[0] * kv.shape[1] // KEY, WIDE)
    return pl.pallas_call(
        stage,
        out_shape=(
            pltpu.HBM(keys, BF),
            jax.ShapeDtypeStruct((2 * kv.shape[0], ROWS), F32),
            jax.ShapeDtypeStruct(queries.shape, BF),
            jax.ShapeDtypeStruct((int(PARTS[0] * keys[0]), WIDE), BF),
        ),
        in_specs=[
            pl.BlockSpec(memory_space=pltpu.HBM),
            pl.BlockSpec(memory_space=pltpu.HBM),
            pl.BlockSpec(memory_space=pltpu.HBM),
            pl.BlockSpec(memory_space=pltpu.SMEM),
        ],
        out_specs=(
            pl.BlockSpec(memory_space=pltpu.HBM),
            pl.BlockSpec(memory_space=pltpu.VMEM),
            pl.BlockSpec(memory_space=pltpu.VMEM),
            pl.BlockSpec(memory_space=pltpu.VMEM),
        ),
        scratch_shapes=[
            pltpu.VMEM(kv.shape, BF),
            pltpu.VMEM(blocks.shape, jnp.int32),
            pltpu.VMEM(keys, BF),
            pltpu.SemaphoreType.DMA((steps + 2,)),
            pltpu.SemaphoreType.DMA((steps,)),
        ],
        compiler_params=pltpu.CompilerParams(vmem_limit_bytes=24 * 2**20),
        interpret=INTERPRET,
    )(in_hbm(kv), in_hbm(blocks), in_hbm(queries), shard)


def attend(q_ref, w_ref, vue_ref, bias_ref, head_ref, k_hbm, out_ref, qt, s_ref, p_ref, k_ref, sems):
    width = qt.shape[1]
    rows = width // H_DEV
    bounds = [0]
    for share in PARTS:
        bounds.append(bounds[-1] + int(share * k_ref.shape[0]))
    spans = list(zip(bounds, bounds[1:]))
    copies = [None]
    for n, (a, b) in enumerate(spans[1:]):
        span = pl.ds(a, b - a)
        copies.append(pltpu.make_async_copy(k_hbm.at[span], k_ref.at[span], sems.at[n]))
        copies[-1].start()
    qt[KEY:, :] = jnp.zeros((WIDE - KEY, width), BF)
    for h in range(H_DEV):
        own = slice(h * rows, (h + 1) * rows)
        q = q_ref[:, h * (NOPE + ROPE) : (h + 1) * (NOPE + ROPE)]
        absorbed = lax.dot_general(
            w_ref[h], q[:, :NOPE], (((0,), (1,)), ((), ())), preferred_element_type=F32
        )
        qt[:KVR, own] = absorbed.astype(BF)
        qt[KVR:KEY, own] = q[:, NOPE:].T

    def keys(a, b, lanes=WIDE):
        return (head_ref if b <= head_ref.shape[0] else k_ref)[a:b, :lanes]

    def score(first, top):
        s = dot(keys(first, first + CHUNK), qt[...])
        for at in range(0, CHUNK, 128):
            piece = s[at : at + 128, :] + jnp.concatenate([bias_ref[...]] * H_DEV, axis=1)
            top = jnp.maximum(top, jnp.max(piece.reshape(16, 8, width), axis=0))
            s_ref[first + at : first + at + 128, :] = piece
        return top

    def weigh(first, top, total):
        for at in range(first, first + CHUNK, 128):
            w = jnp.exp2((s_ref[at : at + 128, :] - top) * COEF)
            total = total + jnp.sum(w.reshape(16, 8, width), axis=0)
            p_ref[at : at + 128, :] = w.astype(BF)
        return total

    lowest = jnp.full((8, width), NEG, F32)
    tops, totals, accs = [], [], []
    top = lowest
    for first in range(spans[0][0], spans[0][1], CHUNK):
        top = score(first, top)
    tops.append(jnp.max(top, axis=0, keepdims=True))
    for n, (a, b) in enumerate(spans):
        total = jnp.zeros((8, width), F32)
        top = lowest
        now = list(range(a, b, CHUNK))
        later = []
        if n + 1 < len(spans):
            copies[n + 1].wait()
            later = list(range(spans[n + 1][0], spans[n + 1][1], CHUNK))
        while now or later:
            if later:
                top = score(later.pop(0), top)
            if now:
                total = weigh(now.pop(0), tops[n], total)
        if n + 1 < len(spans):
            tops.append(jnp.max(top, axis=0, keepdims=True))
        totals.append(jnp.sum(total, axis=0, keepdims=True))
        accs.append(tn_dot(p_ref[a:b, :], keys(a, b, KVR)))
    top = tops[0]
    for t in tops[1:]:
        top = jnp.maximum(top, t)
    acc, total = 0.0, 0.0
    for a, t, l in zip(accs, tops, totals):
        f = jnp.exp2((t - top) * COEF)
        acc = acc + a * f.reshape(width, 1)
        total = total + f * l
    acc = acc.astype(BF)
    line = lax.broadcasted_iota(jnp.int32, (128, rows), 0)
    tail = jnp.zeros((128, rows), F32)
    for h in range(H_DEV):
        own = slice(h * rows, (h + 1) * rows)
        out_ref[:, h * VD : (h + 1) * VD] = dot(acc[own], vue_ref[h]).astype(BF)
        for k, row in enumerate(pieces(top[:, own], 3) + pieces(total[:, own], 2)):
            tail = jnp.where(line == 8 * h + k, row, tail)
    out_ref[:, H_DEV * VD :] = tail.T.astype(BF)


def merge(parts, tails):
    nums, tops, totals = [], [], []
    for h in range(H_DEV):
        stats = [stats_of(t, h) for t in tails]
        top = stats[0][0]
        for m, _ in stats[1:]:
            top = jnp.maximum(top, m)
        num, total = 0.0, 0.0
        for part, (m, l) in zip(parts, stats):
            f = jnp.exp2((m - top) * COEF)
            num = num + part[:, h * VD : (h + 1) * VD] * f
            total = total + l * f
        nums.append(num)
        tops.append(top)
        totals.append(total)
    return nums, tops, totals


def merge_half(in_ref, out_ref):
    n, rows, _ = in_ref.shape
    data = [in_ref[s].astype(F32) for s in range(n)]
    nums, tops, totals = merge([d[:, : H_DEV * VD] for d in data], [d[:, H_DEV * VD :] for d in data])
    out_ref[...] = jnp.concatenate(nums + [with_stats(tops, totals, rows)], axis=1).astype(BF)


def copies_of_both(own_ref, other_ref, place_ref, out_ref):
    own, other = own_ref[...].astype(F32), other_ref[...].astype(F32)
    lower = place_ref[1] == 0
    first, second = jnp.where(lower, own, other), jnp.where(lower, other, own)
    both = jnp.concatenate([first, second], axis=0).astype(BF)
    for k in range(out_ref.shape[0]):
        out_ref[k] = both


def merge_all(own_ref, other_ref, out_ref):
    data = [own_ref[...].astype(F32), other_ref[...].astype(F32)]
    nums, _, totals = merge([d[:, : H_DEV * VD] for d in data], [d[:, H_DEV * VD :] for d in data])
    value = jnp.concatenate([n / t for n, t in zip(nums, totals)], axis=1).astype(BF)
    for k in range(out_ref.shape[0]):
        out_ref[k] = value


def project(value_ref, w_ref, out_ref):
    res = nt_dot(value_ref[...], w_ref[...])
    order = [res[(c * 8 + xz) * 8 : (c * 8 + xz) * 8 + 8] for xz in range(8) for c in range(2)]
    out_ref[...] = jnp.concatenate(order, axis=0).astype(BF)


def call(kernel, out_shape, *args, scratch=(), spaces=None, limit=16):
    return pl.pallas_call(
        kernel,
        out_shape=out_shape,
        in_specs=[pl.BlockSpec(memory_space=m) for m in spaces or [pltpu.VMEM] * len(args)],
        out_specs=pl.BlockSpec(memory_space=pltpu.VMEM),
        scratch_shapes=list(scratch),
        compiler_params=pltpu.CompilerParams(vmem_limit_bytes=limit * 2**20),
        interpret=INTERPRET,
    )(*args)


def body(queries, w_uk, value_up_weight, w_out, kv_cache, blocks):
    n_ctx = lax.axis_size("ctx")
    n_half = n_ctx // 2
    own = 2 * queries.shape[0]
    shard = lax.axis_index("ctx")
    place = jnp.stack([shard, (shard // 2) % 2]).astype(jnp.int32)
    other = lax.ppermute(queries, "ctx", OTHER_HALF)
    keys, bias, queries, head = staged(kv_cache, blocks.T, queries, place)
    other, bias = lax.optimization_barrier((other, bias))
    both = call(
        copies_of_both,
        jax.ShapeDtypeStruct((n_half, own, queries.shape[1]), BF),
        queries, other, place,
        spaces=[pltpu.VMEM] * 2 + [pltpu.SMEM],
    )
    q = lax.all_to_all(both, "ctx", 0, 0, axis_index_groups=SAME_HALF).reshape(ROWS, -1)
    width = H_DEV * ROWS
    parts = call(
        attend,
        jax.ShapeDtypeStruct((ROWS, WIDE), BF),
        q, w_uk, value_up_weight, bias, head, in_hbm(keys),
        scratch=[
            pltpu.VMEM((WIDE, width), BF),
            pltpu.VMEM((keys.shape[0], width), F32),
            pltpu.VMEM((keys.shape[0], width), BF),
            pltpu.VMEM(keys.shape, BF),
            pltpu.SemaphoreType.DMA((len(PARTS) - 1,)),
        ],
        spaces=[pltpu.VMEM] * 5 + [pltpu.HBM],
        limit=40,
    )
    parts = lax.all_to_all(
        parts.reshape(n_half, own, WIDE), "ctx", 0, 0, axis_index_groups=SAME_HALF
    )
    half = call(merge_half, jax.ShapeDtypeStruct((own, WIDE), BF), parts)
    other = lax.ppermute(half, "ctx", OTHER_HALF)
    value = call(merge_all, jax.ShapeDtypeStruct((n_half, own, H_DEV * VD), BF), half, other)
    value = lax.all_to_all(value, "ctx", 0, 0, axis_index_groups=SAME_HALF).reshape(ROWS, -1)
    partial = call(project, jax.ShapeDtypeStruct((ROWS, w_out.shape[1]), BF), value, w_out.T)
    n_head = lax.axis_size("head")
    shares = lax.all_to_all(partial.reshape(n_head, ROWS // n_head, -1), "head", 0, 0)
    return jnp.sum(shares.astype(F32), axis=0).astype(BF)


def solution(mesh):
    return jax.shard_map(
        body,
        mesh=mesh,
        in_specs=(
            P("ctx", "head"),
            P("head", None, None),
            P("head", None, None),
            P("head", "ctx"),
            P("ctx", None),
            P(),
        ),
        out_specs=P("head", "ctx"),
        check_vma=False,
    )
```

```python
import numpy as np
import jax
import jax.numpy as jnp
from jax import lax
from jax.experimental import pallas as pl
from jax.experimental.pallas import tpu as pltpu
from jax.sharding import PartitionSpec as P

BF = jnp.bfloat16
F32 = jnp.float32
NEG = -1e30
H_DEV = 4
ROWS = 128
NOPE = 128
ROPE = 64
KVR = 512
VD = 128
BLOCK = 64
WIDE = 640
PAIR = 1152
PARTS = (0.375, 0.3125, 0.3125)
CHUNK = 256
STAGE_PAIRS = 4
COEF = float((NOPE + ROPE) ** -0.5 * np.log2(np.e))
INTERPRET = False
KEY = KVR + ROPE

SAME_HALF = [[x * 4 + z * 2 + c for c in range(2) for x in range(4)] for z in range(2)]
OTHER_HALF = [(i, i ^ 2) for i in range(16)]


def nt_dot(a, b):
    return lax.dot_general(a, b, (((1,), (1,)), ((), ())), preferred_element_type=F32)


def dot(a, b):
    return jnp.dot(a, b, preferred_element_type=F32)


def tn_dot(a, b):
    return lax.dot_general(a, b, (((0,), (0,)), ((), ())), preferred_element_type=F32)


def pieces(x, n):
    out = []
    for _ in range(n):
        part = x.astype(BF).astype(F32)
        out.append(part)
        x = x - part
    return out


def with_stats(tops, totals, rows):
    lane = lax.broadcasted_iota(jnp.int32, (rows, 128), 1)
    tail = jnp.zeros((rows, 128), F32)
    for h in range(H_DEV):
        cols = pieces(tops[h], 3) + pieces(totals[h], 2)
        for k, col in enumerate(cols):
            tail = jnp.where(lane == 8 * h + k, col, tail)
    return tail


def stats_of(tail, h):
    t = tail[:, 8 * h : 8 * h + 8]
    top = t[:, 0:1] + (t[:, 1:2] + t[:, 2:3])
    return top, t[:, 3:4] + t[:, 4:5]


def in_hbm(x):
    return pltpu.with_memory_space_constraint(x, pltpu.HBM)


def stage(
    kv_hbm, blocks_hbm, q_hbm, shard_ref, out_hbm, bias_ref, q_ref, head_ref, kv_ref, blocks_ref, keys_ref,
    sems, sent,
):
    count, lanes = kv_ref.shape
    span = STAGE_PAIRS * PAIR
    chunk = STAGE_PAIRS * 2 * count
    steps = lanes // span
    got = []
    for i in range(steps):
        at = pl.ds(i * span, span)
        got.append(pltpu.make_async_copy(kv_hbm.at[:, at], kv_ref.at[:, at], sems.at[i]))
        got[-1].start()
    table = pltpu.make_async_copy(blocks_hbm, blocks_ref, sems.at[steps])
    table.start()
    own = pltpu.make_async_copy(q_hbm, q_ref, sems.at[steps + 1])
    own.start()
    pad = jnp.zeros((count, WIDE - KEY), BF)
    put = []
    for i in range(steps):
        got[i].wait()
        for t in range(STAGE_PAIRS):
            pair = kv_ref[:, i * span + t * PAIR : i * span + (t + 1) * PAIR]
            for o in range(2):
                key = jnp.concatenate([pair[:, o * KEY : (o + 1) * KEY], pad], axis=1)
                first = i * chunk + (2 * t + o) * count
                keys_ref[first : first + count, :] = key
                if first < head_ref.shape[0]:
                    head_ref[first : first + count, :] = key
        at = pl.ds(i * chunk, chunk)
        put.append(pltpu.make_async_copy(keys_ref.at[at], out_hbm.at[at], sent.at[i]))
        put[-1].start()
    table.wait()
    b = blocks_ref[...]
    n = ROWS // 16
    order = [xz * 2 + c for c in range(2) for xz in range(8)]
    b = jnp.concatenate([b[:, k * n : (k + 1) * n] for k in order], axis=1)
    b = b - shard_ref[0] * count
    line = lax.broadcasted_iota(jnp.int32, (count, ROWS), 0)
    bias = jnp.full((count, ROWS), NEG, F32)
    for k in range(b.shape[0]):
        bias = jnp.where(b[k : k + 1, :] == line, 0.0, bias)
    bias_ref[...] = jnp.concatenate([bias, bias], axis=0)
    own.wait()
    for copy in put:
        copy.wait()


def staged(kv, blocks, queries, shard):
    steps = kv.shape[1] // (PAIR * STAGE_PAIRS)
    keys = (kv.shape[0] * kv.shape[1] // KEY, WIDE)
    return pl.pallas_call(
        stage,
        out_shape=(
            pltpu.HBM(keys, BF),
            jax.ShapeDtypeStruct((2 * kv.shape[0], ROWS), F32),
            jax.ShapeDtypeStruct(queries.shape, BF),
            jax.ShapeDtypeStruct((int(PARTS[0] * keys[0]), WIDE), BF),
        ),
        in_specs=[
            pl.BlockSpec(memory_space=pltpu.HBM),
            pl.BlockSpec(memory_space=pltpu.HBM),
            pl.BlockSpec(memory_space=pltpu.HBM),
            pl.BlockSpec(memory_space=pltpu.SMEM),
        ],
        out_specs=(
            pl.BlockSpec(memory_space=pltpu.HBM),
            pl.BlockSpec(memory_space=pltpu.VMEM),
            pl.BlockSpec(memory_space=pltpu.VMEM),
            pl.BlockSpec(memory_space=pltpu.VMEM),
        ),
        scratch_shapes=[
            pltpu.VMEM(kv.shape, BF),
            pltpu.VMEM(blocks.shape, jnp.int32),
            pltpu.VMEM(keys, BF),
            pltpu.SemaphoreType.DMA((steps + 2,)),
            pltpu.SemaphoreType.DMA((steps,)),
        ],
        compiler_params=pltpu.CompilerParams(vmem_limit_bytes=24 * 2**20),
        interpret=INTERPRET,
    )(in_hbm(kv), in_hbm(blocks), in_hbm(queries), shard)


def attend(q_ref, w_ref, vue_ref, bias_ref, head_ref, k_hbm, out_ref, qt, s_ref, p_ref, k_ref, sems):
    width = qt.shape[1]
    rows = width // H_DEV
    bounds = [0]
    for share in PARTS:
        bounds.append(bounds[-1] + int(share * k_ref.shape[0]))
    spans = list(zip(bounds, bounds[1:]))
    copies = [None]
    for n, (a, b) in enumerate(spans[1:]):
        span = pl.ds(a, b - a)
        copies.append(pltpu.make_async_copy(k_hbm.at[span], k_ref.at[span], sems.at[n]))
        copies[-1].start()
    qt[KEY:, :] = jnp.zeros((WIDE - KEY, width), BF)
    for h in range(H_DEV):
        own = slice(h * rows, (h + 1) * rows)
        q = q_ref[:, h * (NOPE + ROPE) : (h + 1) * (NOPE + ROPE)]
        absorbed = lax.dot_general(
            w_ref[h], q[:, :NOPE], (((0,), (1,)), ((), ())), preferred_element_type=F32
        )
        qt[:KVR, own] = absorbed.astype(BF)
        qt[KVR:KEY, own] = q[:, NOPE:].T

    def keys(a, b, lanes=WIDE):
        return (head_ref if b <= head_ref.shape[0] else k_ref)[a:b, :lanes]

    def score(first, top):
        s = dot(keys(first, first + CHUNK), qt[...])
        for at in range(0, CHUNK, 128):
            piece = s[at : at + 128, :] + jnp.concatenate([bias_ref[...]] * H_DEV, axis=1)
            top = jnp.maximum(top, jnp.max(piece.reshape(16, 8, width), axis=0))
            s_ref[first + at : first + at + 128, :] = piece
        return top

    def weigh(first, top, total):
        for at in range(first, first + CHUNK, 128):
            w = jnp.exp2((s_ref[at : at + 128, :] - top) * COEF)
            total = total + jnp.sum(w.reshape(16, 8, width), axis=0)
            p_ref[at : at + 128, :] = w.astype(BF)
        return total

    lowest = jnp.full((8, width), NEG, F32)
    tops, totals, accs = [], [], []
    top = lowest
    for first in range(spans[0][0], spans[0][1], CHUNK):
        top = score(first, top)
    tops.append(jnp.max(top, axis=0, keepdims=True))
    for n, (a, b) in enumerate(spans):
        total = jnp.zeros((8, width), F32)
        top = lowest
        now = list(range(a, b, CHUNK))
        later = []
        if n + 1 < len(spans):
            copies[n + 1].wait()
            later = list(range(spans[n + 1][0], spans[n + 1][1], CHUNK))
        while now or later:
            if later:
                top = score(later.pop(0), top)
            if now:
                total = weigh(now.pop(0), tops[n], total)
        if n + 1 < len(spans):
            tops.append(jnp.max(top, axis=0, keepdims=True))
        totals.append(jnp.sum(total, axis=0, keepdims=True))
        accs.append(tn_dot(p_ref[a:b, :], keys(a, b, KVR)))
    top = tops[0]
    for t in tops[1:]:
        top = jnp.maximum(top, t)
    acc, total = 0.0, 0.0
    for a, t, l in zip(accs, tops, totals):
        f = jnp.exp2((t - top) * COEF)
        acc = acc + a * f.reshape(width, 1)
        total = total + f * l
    acc = acc.astype(BF)
    line = lax.broadcasted_iota(jnp.int32, (128, rows), 0)
    tail = jnp.zeros((128, rows), F32)
    for h in range(H_DEV):
        own = slice(h * rows, (h + 1) * rows)
        out_ref[:, h * VD : (h + 1) * VD] = dot(acc[own], vue_ref[h]).astype(BF)
        for k, row in enumerate(pieces(top[:, own], 3) + pieces(total[:, own], 2)):
            tail = jnp.where(line == 8 * h + k, row, tail)
    out_ref[:, H_DEV * VD :] = tail.T.astype(BF)


def merge(parts, tails):
    nums, tops, totals = [], [], []
    for h in range(H_DEV):
        stats = [stats_of(t, h) for t in tails]
        top = stats[0][0]
        for m, _ in stats[1:]:
            top = jnp.maximum(top, m)
        num, total = 0.0, 0.0
        for part, (m, l) in zip(parts, stats):
            f = jnp.exp2((m - top) * COEF)
            num = num + part[:, h * VD : (h + 1) * VD] * f
            total = total + l * f
        nums.append(num)
        tops.append(top)
        totals.append(total)
    return nums, tops, totals


def merge_half(in_ref, out_ref):
    n, rows, _ = in_ref.shape
    data = [in_ref[s].astype(F32) for s in range(n)]
    nums, tops, totals = merge([d[:, : H_DEV * VD] for d in data], [d[:, H_DEV * VD :] for d in data])
    out_ref[...] = jnp.concatenate(nums + [with_stats(tops, totals, rows)], axis=1).astype(BF)


def copies_of_both(own_ref, other_ref, place_ref, out_ref):
    own, other = own_ref[...].astype(F32), other_ref[...].astype(F32)
    lower = place_ref[1] == 0
    first, second = jnp.where(lower, own, other), jnp.where(lower, other, own)
    both = jnp.concatenate([first, second], axis=0).astype(BF)
    for k in range(out_ref.shape[0]):
        out_ref[k] = both


def merge_all(own_ref, other_ref, out_ref):
    data = [own_ref[...].astype(F32), other_ref[...].astype(F32)]
    nums, _, totals = merge([d[:, : H_DEV * VD] for d in data], [d[:, H_DEV * VD :] for d in data])
    value = jnp.concatenate([n / t for n, t in zip(nums, totals)], axis=1).astype(BF)
    for k in range(out_ref.shape[0]):
        out_ref[k] = value


def project(value_ref, w_ref, out_ref):
    res = nt_dot(value_ref[...], w_ref[...])
    order = [res[(c * 8 + xz) * 8 : (c * 8 + xz) * 8 + 8] for xz in range(8) for c in range(2)]
    out_ref[...] = jnp.concatenate(order, axis=0).astype(BF)


def call(kernel, out_shape, *args, scratch=(), spaces=None, limit=16):
    return pl.pallas_call(
        kernel,
        out_shape=out_shape,
        in_specs=[pl.BlockSpec(memory_space=m) for m in spaces or [pltpu.VMEM] * len(args)],
        out_specs=pl.BlockSpec(memory_space=pltpu.VMEM),
        scratch_shapes=list(scratch),
        compiler_params=pltpu.CompilerParams(vmem_limit_bytes=limit * 2**20),
        interpret=INTERPRET,
    )(*args)


def body(queries, w_uk, value_up_weight, w_out, kv_cache, blocks):
    n_ctx = lax.axis_size("ctx")
    n_half = n_ctx // 2
    own = 2 * queries.shape[0]
    shard = lax.axis_index("ctx")
    place = jnp.stack([shard, (shard // 2) % 2]).astype(jnp.int32)
    other = lax.ppermute(queries, "ctx", OTHER_HALF)
    keys, bias, queries, head = staged(kv_cache, blocks.T, queries, place)
    other, bias = lax.optimization_barrier((other, bias))
    both = call(
        copies_of_both,
        jax.ShapeDtypeStruct((n_half, own, queries.shape[1]), BF),
        queries, other, place,
        spaces=[pltpu.VMEM] * 2 + [pltpu.SMEM],
    )
    q = lax.all_to_all(both, "ctx", 0, 0, axis_index_groups=SAME_HALF).reshape(ROWS, -1)
    width = H_DEV * ROWS
    parts = call(
        attend,
        jax.ShapeDtypeStruct((ROWS, WIDE), BF),
        q, w_uk, value_up_weight, bias, head, in_hbm(keys),
        scratch=[
            pltpu.VMEM((WIDE, width), BF),
            pltpu.VMEM((keys.shape[0], width), F32),
            pltpu.VMEM((keys.shape[0], width), BF),
            pltpu.VMEM(keys.shape, BF),
            pltpu.SemaphoreType.DMA((len(PARTS) - 1,)),
        ],
        spaces=[pltpu.VMEM] * 5 + [pltpu.HBM],
        limit=40,
    )
    parts = lax.all_to_all(
        parts.reshape(n_half, own, WIDE), "ctx", 0, 0, axis_index_groups=SAME_HALF
    )
    half = call(merge_half, jax.ShapeDtypeStruct((own, WIDE), BF), parts)
    other = lax.ppermute(half, "ctx", OTHER_HALF)
    value = call(merge_all, jax.ShapeDtypeStruct((n_half, own, H_DEV * VD), BF), half, other)
    value = lax.all_to_all(value, "ctx", 0, 0, axis_index_groups=SAME_HALF).reshape(ROWS, -1)
    partial = call(project, jax.ShapeDtypeStruct((ROWS, w_out.shape[1]), BF), value, w_out.T)
    n_head = lax.axis_size("head")
    shares = lax.all_to_all(partial.reshape(n_head, ROWS // n_head, -1), "head", 0, 0)
    return jnp.sum(shares.astype(F32), axis=0).astype(BF)


def solution(mesh):
    return jax.shard_map(
        body,
        mesh=mesh,
        in_specs=(
            P("ctx", "head"),
            P("head", None, None),
            P("head", None, None),
            P("head", "ctx"),
            P("ctx", None),
            P(),
        ),
        out_specs=P("head", "ctx"),
        check_vma=False,
    )
```

```python
import numpy as np
import jax
import jax.numpy as jnp
from jax import lax
from jax.experimental import pallas as pl
from jax.experimental.pallas import tpu as pltpu
from jax.sharding import PartitionSpec as P

BF = jnp.bfloat16
F32 = jnp.float32
NEG = -1e30
H_DEV = 4
ROWS = 128
NOPE = 128
ROPE = 64
KVR = 512
VD = 128
BLOCK = 64
WIDE = 640
PAIR = 1152
PARTS = (0.5, 0.25, 0.25)
CHUNK = 256
STAGE_PAIRS = 4
COEF = float((NOPE + ROPE) ** -0.5 * np.log2(np.e))
INTERPRET = False
KEY = KVR + ROPE

SAME_HALF = [[x * 4 + z * 2 + c for c in range(2) for x in range(4)] for z in range(2)]
OTHER_HALF = [(i, i ^ 2) for i in range(16)]


def nt_dot(a, b):
    return lax.dot_general(a, b, (((1,), (1,)), ((), ())), preferred_element_type=F32)


def dot(a, b):
    return jnp.dot(a, b, preferred_element_type=F32)


def tn_dot(a, b):
    return lax.dot_general(a, b, (((0,), (0,)), ((), ())), preferred_element_type=F32)


def pieces(x, n):
    out = []
    for _ in range(n):
        part = x.astype(BF).astype(F32)
        out.append(part)
        x = x - part
    return out


def with_stats(tops, totals, rows):
    lane = lax.broadcasted_iota(jnp.int32, (rows, 128), 1)
    tail = jnp.zeros((rows, 128), F32)
    for h in range(H_DEV):
        cols = pieces(tops[h], 3) + pieces(totals[h], 2)
        for k, col in enumerate(cols):
            tail = jnp.where(lane == 8 * h + k, col, tail)
    return tail


def stats_of(tail, h):
    t = tail[:, 8 * h : 8 * h + 8]
    top = t[:, 0:1] + (t[:, 1:2] + t[:, 2:3])
    return top, t[:, 3:4] + t[:, 4:5]


def in_hbm(x):
    return pltpu.with_memory_space_constraint(x, pltpu.HBM)


def stage(
    kv_hbm, blocks_hbm, q_hbm, shard_ref, out_hbm, bias_ref, q_ref, head_ref, kv_ref, blocks_ref, keys_ref,
    sems, sent,
):
    count, lanes = kv_ref.shape
    span = STAGE_PAIRS * PAIR
    chunk = STAGE_PAIRS * 2 * count
    steps = lanes // span
    got = []
    for i in range(steps):
        at = pl.ds(i * span, span)
        got.append(pltpu.make_async_copy(kv_hbm.at[:, at], kv_ref.at[:, at], sems.at[i]))
        got[-1].start()
    table = pltpu.make_async_copy(blocks_hbm, blocks_ref, sems.at[steps])
    table.start()
    own = pltpu.make_async_copy(q_hbm, q_ref, sems.at[steps + 1])
    own.start()
    pad = jnp.zeros((count, WIDE - KEY), BF)
    put = []
    for i in range(steps):
        got[i].wait()
        for t in range(STAGE_PAIRS):
            pair = kv_ref[:, i * span + t * PAIR : i * span + (t + 1) * PAIR]
            for o in range(2):
                key = jnp.concatenate([pair[:, o * KEY : (o + 1) * KEY], pad], axis=1)
                first = i * chunk + (2 * t + o) * count
                keys_ref[first : first + count, :] = key
                if first < head_ref.shape[0]:
                    head_ref[first : first + count, :] = key
        at = pl.ds(i * chunk, chunk)
        put.append(pltpu.make_async_copy(keys_ref.at[at], out_hbm.at[at], sent.at[i]))
        put[-1].start()
    table.wait()
    b = blocks_ref[...]
    n = ROWS // 16
    order = [xz * 2 + c for c in range(2) for xz in range(8)]
    b = jnp.concatenate([b[:, k * n : (k + 1) * n] for k in order], axis=1)
    b = b - shard_ref[0] * count
    line = lax.broadcasted_iota(jnp.int32, (count, ROWS), 0)
    bias = jnp.full((count, ROWS), NEG, F32)
    for k in range(b.shape[0]):
        bias = jnp.where(b[k : k + 1, :] == line, 0.0, bias)
    bias_ref[...] = jnp.concatenate([bias, bias], axis=0)
    own.wait()
    for copy in put:
        copy.wait()


def staged(kv, blocks, queries, shard):
    steps = kv.shape[1] // (PAIR * STAGE_PAIRS)
    keys = (kv.shape[0] * kv.shape[1] // KEY, WIDE)
    return pl.pallas_call(
        stage,
        out_shape=(
            pltpu.HBM(keys, BF),
            jax.ShapeDtypeStruct((2 * kv.shape[0], ROWS), F32),
            jax.ShapeDtypeStruct(queries.shape, BF),
            jax.ShapeDtypeStruct((int(PARTS[0] * keys[0]), WIDE), BF),
        ),
        in_specs=[
            pl.BlockSpec(memory_space=pltpu.HBM),
            pl.BlockSpec(memory_space=pltpu.HBM),
            pl.BlockSpec(memory_space=pltpu.HBM),
            pl.BlockSpec(memory_space=pltpu.SMEM),
        ],
        out_specs=(
            pl.BlockSpec(memory_space=pltpu.HBM),
            pl.BlockSpec(memory_space=pltpu.VMEM),
            pl.BlockSpec(memory_space=pltpu.VMEM),
            pl.BlockSpec(memory_space=pltpu.VMEM),
        ),
        scratch_shapes=[
            pltpu.VMEM(kv.shape, BF),
            pltpu.VMEM(blocks.shape, jnp.int32),
            pltpu.VMEM(keys, BF),
            pltpu.SemaphoreType.DMA((steps + 2,)),
            pltpu.SemaphoreType.DMA((steps,)),
        ],
        compiler_params=pltpu.CompilerParams(vmem_limit_bytes=24 * 2**20),
        interpret=INTERPRET,
    )(in_hbm(kv), in_hbm(blocks), in_hbm(queries), shard)


def attend(q_ref, w_ref, vue_ref, bias_ref, head_ref, k_hbm, out_ref, qt, s_ref, p_ref, k_ref, sems):
    width = qt.shape[1]
    rows = width // H_DEV
    bounds = [0]
    for share in PARTS:
        bounds.append(bounds[-1] + int(share * k_ref.shape[0]))
    spans = list(zip(bounds, bounds[1:]))
    copies = [None]
    for n, (a, b) in enumerate(spans[1:]):
        span = pl.ds(a, b - a)
        copies.append(pltpu.make_async_copy(k_hbm.at[span], k_ref.at[span], sems.at[n]))
        copies[-1].start()
    qt[KEY:, :] = jnp.zeros((WIDE - KEY, width), BF)
    for h in range(H_DEV):
        own = slice(h * rows, (h + 1) * rows)
        q = q_ref[:, h * (NOPE + ROPE) : (h + 1) * (NOPE + ROPE)]
        absorbed = lax.dot_general(
            w_ref[h], q[:, :NOPE], (((0,), (1,)), ((), ())), preferred_element_type=F32
        )
        qt[:KVR, own] = absorbed.astype(BF)
        qt[KVR:KEY, own] = q[:, NOPE:].T

    def keys(a, b, lanes=WIDE):
        return (head_ref if b <= head_ref.shape[0] else k_ref)[a:b, :lanes]

    def score(first, top):
        s = dot(keys(first, first + CHUNK), qt[...])
        for at in range(0, CHUNK, 128):
            piece = s[at : at + 128, :] + jnp.concatenate([bias_ref[...]] * H_DEV, axis=1)
            top = jnp.maximum(top, jnp.max(piece.reshape(16, 8, width), axis=0))
            s_ref[first + at : first + at + 128, :] = piece
        return top

    def weigh(first, top, total):
        for at in range(first, first + CHUNK, 128):
            w = jnp.exp2((s_ref[at : at + 128, :] - top) * COEF)
            total = total + jnp.sum(w.reshape(16, 8, width), axis=0)
            p_ref[at : at + 128, :] = w.astype(BF)
        return total

    lowest = jnp.full((8, width), NEG, F32)
    tops, totals, accs = [], [], []
    top = lowest
    for first in range(spans[0][0], spans[0][1], CHUNK):
        top = score(first, top)
    tops.append(jnp.max(top, axis=0, keepdims=True))
    for n, (a, b) in enumerate(spans):
        total = jnp.zeros((8, width), F32)
        top = lowest
        now = list(range(a, b, CHUNK))
        later = []
        if n + 1 < len(spans):
            copies[n + 1].wait()
            later = list(range(spans[n + 1][0], spans[n + 1][1], CHUNK))
        while now or later:
            if later:
                top = score(later.pop(0), top)
            if now:
                total = weigh(now.pop(0), tops[n], total)
        if n + 1 < len(spans):
            tops.append(jnp.max(top, axis=0, keepdims=True))
        totals.append(jnp.sum(total, axis=0, keepdims=True))
        accs.append(tn_dot(p_ref[a:b, :], keys(a, b, KVR)))
    top = tops[0]
    for t in tops[1:]:
        top = jnp.maximum(top, t)
    acc, total = 0.0, 0.0
    for a, t, l in zip(accs, tops, totals):
        f = jnp.exp2((t - top) * COEF)
        acc = acc + a * f.reshape(width, 1)
        total = total + f * l
    acc = acc.astype(BF)
    line = lax.broadcasted_iota(jnp.int32, (128, rows), 0)
    tail = jnp.zeros((128, rows), F32)
    for h in range(H_DEV):
        own = slice(h * rows, (h + 1) * rows)
        out_ref[:, h * VD : (h + 1) * VD] = dot(acc[own], vue_ref[h]).astype(BF)
        for k, row in enumerate(pieces(top[:, own], 3) + pieces(total[:, own], 2)):
            tail = jnp.where(line == 8 * h + k, row, tail)
    out_ref[:, H_DEV * VD :] = tail.T.astype(BF)


def merge(parts, tails):
    nums, tops, totals = [], [], []
    for h in range(H_DEV):
        stats = [stats_of(t, h) for t in tails]
        top = stats[0][0]
        for m, _ in stats[1:]:
            top = jnp.maximum(top, m)
        num, total = 0.0, 0.0
        for part, (m, l) in zip(parts, stats):
            f = jnp.exp2((m - top) * COEF)
            num = num + part[:, h * VD : (h + 1) * VD] * f
            total = total + l * f
        nums.append(num)
        tops.append(top)
        totals.append(total)
    return nums, tops, totals


def merge_half(in_ref, out_ref):
    n, rows, _ = in_ref.shape
    data = [in_ref[s].astype(F32) for s in range(n)]
    nums, tops, totals = merge([d[:, : H_DEV * VD] for d in data], [d[:, H_DEV * VD :] for d in data])
    out_ref[...] = jnp.concatenate(nums + [with_stats(tops, totals, rows)], axis=1).astype(BF)


def copies_of_both(own_ref, other_ref, place_ref, out_ref):
    own, other = own_ref[...].astype(F32), other_ref[...].astype(F32)
    lower = place_ref[1] == 0
    first, second = jnp.where(lower, own, other), jnp.where(lower, other, own)
    both = jnp.concatenate([first, second], axis=0).astype(BF)
    for k in range(out_ref.shape[0]):
        out_ref[k] = both


def merge_all(own_ref, other_ref, out_ref):
    data = [own_ref[...].astype(F32), other_ref[...].astype(F32)]
    nums, _, totals = merge([d[:, : H_DEV * VD] for d in data], [d[:, H_DEV * VD :] for d in data])
    value = jnp.concatenate([n / t for n, t in zip(nums, totals)], axis=1).astype(BF)
    for k in range(out_ref.shape[0]):
        out_ref[k] = value


def project(value_ref, w_ref, out_ref):
    res = nt_dot(value_ref[...], w_ref[...])
    order = [res[(c * 8 + xz) * 8 : (c * 8 + xz) * 8 + 8] for xz in range(8) for c in range(2)]
    out_ref[...] = jnp.concatenate(order, axis=0).astype(BF)


def call(kernel, out_shape, *args, scratch=(), spaces=None, limit=16):
    return pl.pallas_call(
        kernel,
        out_shape=out_shape,
        in_specs=[pl.BlockSpec(memory_space=m) for m in spaces or [pltpu.VMEM] * len(args)],
        out_specs=pl.BlockSpec(memory_space=pltpu.VMEM),
        scratch_shapes=list(scratch),
        compiler_params=pltpu.CompilerParams(vmem_limit_bytes=limit * 2**20),
        interpret=INTERPRET,
    )(*args)


def body(queries, w_uk, value_up_weight, w_out, kv_cache, blocks):
    n_ctx = lax.axis_size("ctx")
    n_half = n_ctx // 2
    own = 2 * queries.shape[0]
    shard = lax.axis_index("ctx")
    place = jnp.stack([shard, (shard // 2) % 2]).astype(jnp.int32)
    other = lax.ppermute(queries, "ctx", OTHER_HALF)
    keys, bias, queries, head = staged(kv_cache, blocks.T, queries, place)
    other, bias = lax.optimization_barrier((other, bias))
    both = call(
        copies_of_both,
        jax.ShapeDtypeStruct((n_half, own, queries.shape[1]), BF),
        queries, other, place,
        spaces=[pltpu.VMEM] * 2 + [pltpu.SMEM],
    )
    q = lax.all_to_all(both, "ctx", 0, 0, axis_index_groups=SAME_HALF).reshape(ROWS, -1)
    width = H_DEV * ROWS
    parts = call(
        attend,
        jax.ShapeDtypeStruct((ROWS, WIDE), BF),
        q, w_uk, value_up_weight, bias, head, in_hbm(keys),
        scratch=[
            pltpu.VMEM((WIDE, width), BF),
            pltpu.VMEM((keys.shape[0], width), F32),
            pltpu.VMEM((keys.shape[0], width), BF),
            pltpu.VMEM(keys.shape, BF),
            pltpu.SemaphoreType.DMA((len(PARTS) - 1,)),
        ],
        spaces=[pltpu.VMEM] * 5 + [pltpu.HBM],
        limit=40,
    )
    parts = lax.all_to_all(
        parts.reshape(n_half, own, WIDE), "ctx", 0, 0, axis_index_groups=SAME_HALF
    )
    half = call(merge_half, jax.ShapeDtypeStruct((own, WIDE), BF), parts)
    other = lax.ppermute(half, "ctx", OTHER_HALF)
    value = call(merge_all, jax.ShapeDtypeStruct((n_half, own, H_DEV * VD), BF), half, other)
    value = lax.all_to_all(value, "ctx", 0, 0, axis_index_groups=SAME_HALF).reshape(ROWS, -1)
    partial = call(project, jax.ShapeDtypeStruct((ROWS, w_out.shape[1]), BF), value, w_out.T)
    n_head = lax.axis_size("head")
    shares = lax.all_to_all(partial.reshape(n_head, ROWS // n_head, -1), "head", 0, 0)
    return jnp.sum(shares.astype(F32), axis=0).astype(BF)


def solution(mesh):
    return jax.shard_map(
        body,
        mesh=mesh,
        in_specs=(
            P("ctx", "head"),
            P("head", None, None),
            P("head", None, None),
            P("head", "ctx"),
            P("ctx", None),
            P(),
        ),
        out_specs=P("head", "ctx"),
        check_vma=False,
    )
```
